512 devices in a mesh: ctx: 64 (over x, z, core), head: 8 (over y).
Axes of the slice: x: 4, y: 8, z: 8, core: 2. Of those that a mesh axis runs over, the one named last changes fastest.
Arguments:
- hidden: bfloat16 [16384, 4096], P('ctx'), may hold values from -6 to 6
- w_bc: bfloat16 [4096, 2048], P('ctx', 'head'), may hold values from -0.0078125 to 0.0078125
- x_act: bfloat16 [16384, 4096], P('ctx', 'head'), may hold values from -6 to 6
- step_size: float32 [64, 16384], P('head', 'ctx'), may hold values from 0.5 to 1.5
- decay_rate: float32 [64], P('head'), may hold values from 2.4414063e-05 to 0.04
- skip_gain: float32 [64], P('head'), may hold values from 0.5 to 1.5
- logp_dir: bfloat16 [16384, 4096], P('ctx', 'head'), may hold values from -0.29882812 to 0.29882812
- base_logp: float32 [16384], P('ctx'), may hold values from -6 to 6
- seq_stretches: int32 [4], replicated, may hold values from 1 to 32, 64 in all
- resp_mask: int32 [16384], P('ctx'), may hold values 0 or 1
Outputs:
- grad_x: bfloat16 [16384, 4096], P('ctx', 'head')
- grad_step: float32 [64, 16384], P('head', 'ctx')
- grad_rate: float32 [64], P('head')
- grad_skip: float32 [64], P('head')
- grad_w: float32 [4096, 2048], P('ctx', 'head')
The draws below stay inside these ranges and needn't reach their ends.
Inputs may be any that keep to these rules, and one draw needn't show every extreme that they name: Sequences 2p and 2p+1 are pair p's chosen and rejected answers; sequence j holds seq_stretches[j] whole blocks of 256 tokens, and the blocks of all 4 sequences add up to 64; some sequence has exactly 32 blocks.
All inputs are finite; a program needn't handle non-finite values. No bound on the sum of `resp_mask` on one device may be relied on, other than what follows from the above.
Results may differ from the reference program's by a relative error of at most 0.015.
Values may be sent and summed in bfloat16 or wider, within the bound.
A program may use at most 64 MiB of HBM per device.

```python
import math
import jax
import jax.numpy as jnp
import numpy as np
from jax import lax

D = 4096
HEADS = 64
HEADDIM = 64
NSTATE = 128
GROUPS = 8
STRETCH = 256
SEQS = 4
MOST = 32
TOKENS = 16384
N_CTX = 64


def set_ends(values, own_key, least, high):
    index_at = [jax.random.randint(jax.random.fold_in(own_key, axis), (), 0, length) for axis, length in enumerate(values.shape)]
    widest = values.shape.index(max(values.shape))
    beside = index_at[:widest] + [(index_at[widest] + 1) % values.shape[widest]] + index_at[widest + 1:]
    return values.at[tuple(index_at)].set(least).at[tuple(beside)].set(high)


def shard_levels(own_key, shape, shards, least, high):
    def one(position, blocks):
        draws = jax.random.uniform(jax.random.fold_in(jax.random.fold_in(own_key, 6), position), (blocks,), jnp.float32, least / len(shards), high / len(shards))
        return jnp.repeat(jnp.exp(draws), shape[position] // blocks).reshape((-1,) + (1,) * (len(shape) - position - 1))

    factor_of = one(*shards[0])
    for cut in shards[1:]:
        factor_of = factor_of * one(*cut)
    return factor_of


def profile(count, total, most, skew):
    loads = [(1 << 20) // math.isqrt(rank ** skew) + 1 for rank in range(2, count + 1)]
    rest, given = total - most - (count - 1), [1] * (count - 1)
    while rest > 0:
        candidates = [i for i in range(count - 1) if given[i] < most]
        pool, budget = sum([loads[i] for i in candidates]), rest
        for i in candidates:
            extra = min(most - given[i], max(1, budget * loads[i] // pool), rest)
            given[i] = given[i] + extra
            rest = rest - extra
    return np.array([most] + given)


def ragged_sizes(own_key, amount, total, reach, slope):
    if amount == 2:
        one = jax.random.randint(own_key, (), max(1, total - reach), min(reach, total - 1) + 1)
        return jnp.stack([one, total - one])
    tallies = jnp.asarray(profile(amount, total, reach, slope), jnp.int32)
    pairs = (amount - 1) // 2
    source_of, receiver = tallies[1:1 + 2 * pairs:2], tallies[2:2 + 2 * pairs:2]
    room = jnp.minimum(source_of - 1, reach - receiver)
    moved = jax.random.randint(jax.random.fold_in(own_key, 1), (pairs,), 0, 1 << 20) % (room + 1)
    tallies = tallies.at[1:1 + 2 * pairs:2].set(source_of - moved).at[2:2 + 2 * pairs:2].set(receiver + moved)
    return tallies[jax.random.permutation(jax.random.fold_in(own_key, 2), amount)]


def gaussian(own_key, shape, spread, bound, cuts=(), held_as=jnp.bfloat16):
    level = shard_levels(own_key, shape, cuts, -0.22, 0.18) if cuts else 1.0
    result = jax.random.normal(own_key, shape, jnp.float32) * spread * level
    return jnp.minimum(jnp.maximum(result, -bound), bound).astype(held_as)


def setup_inputs(seed: int = 0) -> dict:
    arg_keys = jax.random.split(jax.random.key(seed), 11)
    hidden = gaussian(arg_keys[0], (TOKENS, D), 1.0, 6.0, ((0, 64),))
    w_bc = gaussian(arg_keys[1], (D, GROUPS * 2 * NSTATE), (D * NSTATE) ** -0.5, 0.0078125, ((0, 64), (1, 8)))
    x_act = gaussian(arg_keys[2], (TOKENS, HEADS * HEADDIM), 1.0, 6.0, ((0, 64), (1, 8)))
    step_size = jnp.clip(0.5 + 1.0 * jax.random.uniform(arg_keys[3], (HEADS, TOKENS), jnp.float32) ** shard_levels(arg_keys[3], (HEADS, TOKENS), ((0, 8), (1, 64)), -0.2, 0.2), 0.5, 1.5)
    decay_rate = jnp.clip(jnp.exp(math.log(0.04) - 7.4014754 * jax.random.uniform(arg_keys[4], (HEADS,), jnp.float32) ** shard_levels(arg_keys[4], (HEADS,), ((0, 8),), -0.2, 0.2)), 2.441406286379788e-05, 0.04)
    skip_gain = jnp.clip(0.5 + 1.0 * jax.random.uniform(arg_keys[5], (HEADS,), jnp.float32) ** shard_levels(arg_keys[5], (HEADS,), ((0, 8),), -0.2, 0.2), 0.5, 1.5)
    logp_dir = gaussian(arg_keys[6], (TOKENS, HEADS * HEADDIM), 0.05, 0.29882812, ((0, 64), (1, 8)))
    base_logp = gaussian(arg_keys[7], (TOKENS,), 1.0, 6.0, ((0, 64),), jnp.float32)
    seq_stretches = ragged_sizes(arg_keys[8], SEQS, N_CTX, MOST, 1).astype(jnp.int32)
    resp_mask = set_ends((jax.random.randint(arg_keys[9], (TOKENS,), 0, 4) < 3).astype(jnp.int32), jax.random.fold_in(arg_keys[9], 1), 0, 1)
    return {"hidden": hidden, "w_bc": w_bc, "x_act": x_act, "step_size": step_size, "decay_rate": decay_rate, "skip_gain": skip_gain, "logp_dir": logp_dir, "base_logp": base_logp, "seq_stretches": seq_stretches, "resp_mask": resp_mask}


hinge_sharp = 0.005
hinge_margin = 10.0

def einsum_wide(form, left, right):
    return jnp.einsum(form, left.astype(jnp.float32), right.astype(jnp.float32))

def block_state(inputs, step_group, rate_group, b_input):
    cum_decay = jnp.cumsum(-step_group * rate_group[:, :, None], axis=2)
    last_cum = cum_decay[:, :, -1:]
    factor = jnp.exp(last_cum - cum_decay) * step_group
    b_float = b_input.astype(jnp.float32).transpose(1, 0, 2)
    weighted = (factor[:, :, :, None] * b_float[:, None]).astype(jnp.bfloat16)
    local_state = einsum_wide('tghp,ghtn->ghpn', inputs, weighted)
    block_decay = jnp.exp(last_cum[:, :, 0])
    return (local_state, block_decay, cum_decay)

def block_output(inputs, step_group, cum_decay, skip_group, b_input, c_input, state_in):
    length = inputs.shape[0]
    scores = einsum_wide('tgn,sgn->gts', c_input, b_input)
    row_index = lax.broadcasted_iota(jnp.int32, (length, length), 0)
    col_index = lax.broadcasted_iota(jnp.int32, (length, length), 1)
    causal = row_index >= col_index
    gap_decay = jnp.where(causal, cum_decay[:, :, :, None] - cum_decay[:, :, None, :], 0.0)
    weights = jnp.where(causal, jnp.exp(gap_decay) * scores[:, None] * step_group[:, :, None, :], 0.0)
    weights = weights.astype(jnp.bfloat16)
    within = einsum_wide('ghts,sghp->tghp', weights, inputs)
    carried = jnp.einsum('tgn,ghpn->tghp', c_input.astype(jnp.float32), state_in, precision=lax.Precision.HIGHEST)
    across = carried * jnp.exp(cum_decay).transpose(2, 0, 1)[:, :, :, None]
    return within + across + skip_group[None, :, :, None] * inputs.astype(jnp.float32)

def reference(hidden, w_bc, x_act, step_size, decay_rate, skip_gain, logp_dir, base_logp, seq_stretches, resp_mask):
    block_count = N_CTX
    per_group = HEADS // GROUPS
    projected = jnp.dot(hidden, w_bc, preferred_element_type=jnp.float32).astype(jnp.bfloat16)
    projected = projected.reshape(block_count, STRETCH, GROUPS, 2, NSTATE)
    b_blocks = projected[:, :, :, 0]
    c_blocks = projected[:, :, :, 1]
    seq_ends = jnp.cumsum(seq_stretches)
    seq_starts = seq_ends - seq_stretches
    blocks = jnp.arange(block_count, dtype=jnp.int32)
    block_start = jnp.any(seq_starts[None, :] == blocks[:, None], axis=1)
    seq_of_block = lax.optimization_barrier(jnp.sum((seq_starts[None, :] <= blocks[:, None]).astype(jnp.int32), axis=1)) - 1
    rate_group = decay_rate.reshape(GROUPS, per_group)
    skip_group = skip_gain.reshape(GROUPS, per_group)
    inputs = x_act.reshape(block_count, STRETCH, GROUPS, per_group, HEADDIM)
    step_blocks = step_size.reshape(GROUPS, per_group, block_count, STRETCH).transpose(2, 0, 1, 3)

    def forward(inputs, step_blocks, rate_group, skip_group, b_blocks, c_blocks):

        def block_step(carried, block_item):
            x_block, step_block, b_block, c_block, fresh_flag = block_item
            state_in = jnp.where(fresh_flag, jnp.zeros_like(carried), carried)
            local_state, block_decay, cum_decay = block_state(x_block, step_block, rate_group, b_block)
            y_block = block_output(x_block, step_block, cum_decay, skip_group, b_block, c_block, state_in)
            return (block_decay[:, :, None, None] * state_in + local_state, y_block)
        initial = jnp.zeros((GROUPS, per_group, HEADDIM, NSTATE), jnp.float32)
        _, outputs_all = lax.scan(jax.checkpoint(block_step), initial, (inputs, step_blocks, b_blocks, c_blocks, block_start))
        return outputs_all
    outputs_all, pullback = jax.vjp(forward, inputs, step_blocks, rate_group, skip_group, b_blocks, c_blocks)
    directions = logp_dir.reshape(block_count, STRETCH, GROUPS, per_group, HEADDIM).astype(jnp.float32)
    mask_float = resp_mask.reshape(block_count, STRETCH).astype(jnp.float32)
    token_logp = base_logp.reshape(block_count, STRETCH) + lax.optimization_barrier(jnp.sum(directions * outputs_all, axis=(2, 3, 4)))
    block_sums = lax.optimization_barrier(jnp.sum(mask_float * token_logp, axis=1))
    onehot = (seq_of_block[:, None] == jnp.arange(SEQS, dtype=jnp.int32)[None, :]).astype(jnp.float32)
    seq_sum = jnp.dot(block_sums, onehot, precision=lax.Precision.HIGHEST)
    margins = seq_sum[0::2] - seq_sum[1::2]
    pair_coef = jax.nn.sigmoid(hinge_sharp * (hinge_margin - margins))
    seq_grad = jnp.stack([-pair_coef, pair_coef], axis=1).reshape(SEQS)
    block_grad = jnp.dot(onehot, seq_grad, precision=lax.Precision.HIGHEST)
    cotangent = (mask_float * block_grad[:, None])[:, :, None, None, None] * directions
    grad_x, grad_step, grad_rate, grad_skip, grad_b, grad_c = pullback(cotangent)
    grad_cols = jnp.stack([grad_b, grad_c], axis=3).reshape(TOKENS, GROUPS * 2 * NSTATE)
    grad_w = jnp.dot(hidden.T, grad_cols, preferred_element_type=jnp.float32)
    return (grad_x.reshape(TOKENS, HEADS * HEADDIM), grad_step.transpose(1, 2, 0, 3).reshape(HEADS, TOKENS), grad_rate.reshape(HEADS), grad_skip.reshape(HEADS), grad_w)
```

```python
import functools

import jax
import jax.numpy as jnp
from jax import lax
from jax.experimental import pallas as pl
from jax.experimental.pallas import tpu as pltpu
from jax.sharding import PartitionSpec as P

HEADDIM = 64
NSTATE = 128
NX, NZ, NC = 4, 8, 2
NCTX = NX * NZ * NC
NHEAD = 8
TOK = 256
HEADS = 8
WIDE = HEADS * HEADDIM
DEPTH = 64
COLS = 2 * NSTATE
MODEL = NCTX * DEPTH
PART = 48

hinge_sharp = 0.005
hinge_margin = 10.0

MESH = pl.DeviceIdType.MESH
F32 = jnp.float32
BF16 = jnp.bfloat16
VMEM_LIMIT = 48 << 20


def place():
    index = lax.axis_index("ctx")
    return index // 16, (index // 2) % 8, index % 2, lax.axis_index("head")


def at(x, z, c, head):
    return (((x % NX) * NZ + (z % NZ)) * NC + c, head)


def greet(partners):
    barrier = pltpu.get_barrier_semaphore()
    for partner in partners:
        pl.semaphore_signal(barrier, inc=1, device_id=partner, device_id_type=MESH)
    pl.semaphore_wait(barrier, len(partners))


def plane_partners(x, z, c, head):
    return (
        [at(x, z + dz, c, head) for dz in range(1, NZ)]
        + [at(x + dx, z, c, head) for dx in range(1, NX)]
        + [at(x, z, 1 - c, head)]
    )


def dot(left, right, dims=((1,), (0,)), precision=None):
    return lax.dot_general(left, right, (dims, ((), ())), precision=precision, preferred_element_type=F32)


def gather_kernel(w_ref, step_ref, rate_ref, hid_ref, bc_ref, dec_ref, buf, hid, load_sem, ss, rs):
    x, z, c, head = place()
    load = pltpu.make_async_copy(hid_ref, hid, load_sem)
    load.start()
    greet(plane_partners(x, z, c, head))
    buf[x, z, c] = w_ref[...]
    rows = lax.broadcasted_iota(jnp.int32, (8, 128), 0)
    lanes = lax.broadcasted_iota(jnp.int32, (8, 128), 1)
    total = jnp.sum(step_ref[...], axis=1, keepdims=True)
    spread = jnp.zeros((8, 128), F32)
    for h in range(HEADS):
        spread = jnp.where((rows == h) & (lanes == h), -rate_ref[h] * total, spread)
    dec_ref[x, z, c] = jnp.sum(spread, axis=0, keepdims=True)

    started = []

    def send(ref, index, k, partner):
        piece = ref.at[index]
        copy = pltpu.make_async_remote_copy(
            piece, piece, ss.at[k], rs.at[k], device_id=partner, device_id_type=MESH
        )
        copy.start()
        started.append(copy)

    def arrive(ref, index, k):
        piece = ref.at[index]
        pltpu.make_async_remote_copy(
            piece, piece, ss.at[k], rs.at[k], device_id=at(x, z, 1 - c, head), device_id_type=MESH
        ).wait_recv()

    every = slice(None)
    low, high = pl.ds(0, PART), pl.ds(PART, DEPTH - PART)
    for dz in (4, 3, 5, 2, 6, 1, 7):
        send(buf, (x, z, c, low), dz - 1, at(x, z + dz, c, head))
        send(dec_ref, (x, z, c), 24 + dz, at(x, z + dz, c, head))
    for dx in (2, 1, 3):
        send(buf, (x, z, c, high), 6 + dx, at(x + dx, z, c, head))
    for dz in range(1, NZ):
        arrive(buf, (x, (z - dz) % NZ, c, low), dz - 1)
    for dx in (2, 1, 3):
        send(buf, (x, every, c, low), 9 + dx, at(x + dx, z, c, head))
    for dx in range(1, NX):
        arrive(buf, ((x - dx) % NX, z, c, high), 6 + dx)
    for dz in (4, 3, 5, 2, 6, 1, 7):
        send(buf, (every, z, c, high), 12 + dz, at(x, z + dz, c, head))
    send(buf, (x, every, c, low), 20, at(x, z, 1 - c, head))
    for dz in range(1, NZ):
        arrive(dec_ref, (x, (z - dz) % NZ, c), 24 + dz)
    for dx in range(1, NX):
        send(dec_ref, (x, every, c), 31 + dx, at(x + dx, z, c, head))
    for dz in range(1, NZ):
        arrive(buf, (every, (z - dz) % NZ, c, high), 12 + dz)
    send(buf, (every, every, c, high), 24, at(x, z, 1 - c, head))
    for dx in (1, 3, 2):
        arrive(buf, ((x - dx) % NX, every, c, low), 9 + dx)
        send(buf, ((x - dx) % NX, every, c, low), 20 + dx, at(x, z, 1 - c, head))
    for dx in range(1, NX):
        arrive(dec_ref, ((x - dx) % NX, every, c), 31 + dx)
    send(dec_ref, (every, every, c), 35, at(x, z, 1 - c, head))
    load.wait()
    arrive(buf, (every, every, 1 - c, high), 24)
    arrive(buf, (x, every, 1 - c, low), 20)
    for dx in (1, 3, 2):
        arrive(buf, ((x - dx) % NX, every, 1 - c, low), 20 + dx)
    span = MODEL // NX
    sums = jnp.zeros((TOK, COLS), F32)
    for part in range(NX):
        sums = sums + dot(hid[:, part * span : (part + 1) * span], buf[part].reshape(span, COLS))
    bc_ref[...] = sums.astype(BF16)
    arrive(dec_ref, (every, every, 1 - c), 35)
    for copy in started:
        copy.wait_send()


def gather(w_bc, step_size, decay_rate, hidden):
    vmem = pl.BlockSpec(memory_space=pltpu.VMEM)
    return pl.pallas_call(
        gather_kernel,
        name="gather_project",
        out_shape=(
            jax.ShapeDtypeStruct((TOK, COLS), BF16),
            jax.ShapeDtypeStruct((NX, NZ, NC, 1, 128), F32),
        ),
        in_specs=[
            vmem,
            vmem,
            pl.BlockSpec(memory_space=pltpu.SMEM),
            pl.BlockSpec(memory_space=pl.ANY),
        ],
        out_specs=(vmem, vmem),
        scratch_shapes=[
            pltpu.VMEM((NX, NZ, NC, DEPTH, COLS), BF16),
            pltpu.VMEM((TOK, MODEL), BF16),
            pltpu.SemaphoreType.DMA,
            pltpu.SemaphoreType.DMA((36,)),
            pltpu.SemaphoreType.DMA((36,)),
        ],
        compiler_params=pltpu.CompilerParams(
            collective_id=0, has_side_effects=True, vmem_limit_bytes=VMEM_LIMIT
        ),
    )(w_bc, step_size, decay_rate, hidden)


def pair_columns(columns, base, pair, low_half):
    one, two = base + 2 * pair, base + 2 * pair + 1
    return jnp.where(low_half, columns[:, one : one + 1], columns[:, two : two + 1])


def sequence_starts(stretch_ref):
    one = stretch_ref[0]
    two = one + stretch_ref[1]
    return one, two, two + stretch_ref[2]


def local_kernel(
    bc_ref, x_ref, dir_ref, step_ref, mask_ref, base_ref, dec_ref, rate_ref, skip_ref, stretch_ref,
    msg_ref, tab_ref, own_ref, gbc_ref, gx_ref, rows_ref, cols_ref, xf_ref, dyg_ref, small_ref,
    stack, drow,
):
    index, head = lax.axis_index("ctx"), lax.axis_index("head")
    step = step_ref[...]
    row8 = lax.broadcasted_iota(jnp.int32, (8, TOK), 0)
    rate = jnp.zeros((8, TOK), F32)
    for h in range(HEADS):
        rate = jnp.where(row8 == h, rate_ref[h], rate)
    s_index = lax.broadcasted_iota(jnp.int32, (TOK, TOK), 0)
    t_index = lax.broadcasted_iota(jnp.int32, (TOK, TOK), 1)
    causal = s_index <= t_index
    cum = -rate * dot(step, causal.astype(F32), precision=lax.Precision.HIGHEST)
    last = cum[:, TOK - 1 : TOK]
    mask = mask_ref[...].astype(F32)
    stack[...] = jnp.zeros((128, TOK), F32)
    stack[0:8] = cum - jnp.log(step)
    stack[8:16] = jnp.exp(cum)
    stack[16:24] = jnp.exp(last - cum) * step
    stack[24:32] = jnp.broadcast_to(mask, (8, TOK))
    columns = stack[...].T
    cols_ref[...] = columns
    rows_ref[0:8] = cum

    bc = bc_ref[...]
    b_in, c_in = bc[:, :NSTATE], bc[:, NSTATE:]
    low_half = lax.broadcasted_iota(jnp.int32, (TOK, 128), 1) < HEADDIM
    mask_column = columns[:, 24:25]
    scores = dot(b_in, c_in, ((1,), (1,)))
    grad_scores = jnp.zeros((TOK, TOK), F32)
    back = jnp.zeros((TOK, 128), F32)
    lane128 = lax.broadcasted_iota(jnp.int32, (TOK, 128), 1)
    overlap = []
    for pair in range(HEADS // 2):
        span = slice(128 * pair, 128 * pair + 128)
        x_pair = x_ref[:, span]
        x_wide = x_pair.astype(F32)
        dy_wide = dir_ref[:, span].astype(F32) * mask_column
        dy_pair = dy_wide.astype(BF16)
        xf_ref[:, span] = (x_wide * pair_columns(columns, 16, pair, low_half)).astype(BF16)
        dyg_ref[:, span] = (dy_wide * pair_columns(columns, 8, pair, low_half)).astype(BF16)
        overlap.append(jnp.sum(x_wide * dy_wide, axis=0, keepdims=True))
        within = []
        for h in (2 * pair, 2 * pair + 1):
            half = slice(HEADDIM * (h % 2), HEADDIM * (h % 2) + HEADDIM)
            x_h, dy_h = x_pair[:, half], dy_pair[:, half]
            gap = jnp.where(causal, cum[h : h + 1, :] - columns[:, h : h + 1], -1e30)
            factor = jnp.exp(gap)
            moved = dot(x_h, dy_h, ((1,), (1,))) * factor
            grad_scores = grad_scores + moved
            spent = moved * scores
            drow[h : h + 1] = jnp.sum(spent, axis=0, keepdims=True)
            back = jnp.where(lane128 == h, jnp.sum(spent, axis=1, keepdims=True), back)
            within.append(dot((scores * factor).astype(BF16), dy_h))
        skip_pair = jnp.where(low_half, skip_ref[2 * pair], skip_ref[2 * pair + 1])
        gx_ref[:, span] = jnp.concatenate(within, axis=1) + skip_pair * dy_wide
    rows_ref[8:16] = drow[...]
    rows_ref[16:24] = back.T[0:8]
    local = dot(xf_ref[...], b_in, ((0,), (0,)))
    grown = dot(dyg_ref[...], c_in, ((0,), (0,)))
    msg_ref[...] = jnp.concatenate(
        [local.reshape(NCTX, 8, 128), grown.reshape(NCTX, 8, 128)], axis=1
    ).astype(BF16)
    grad_bf = grad_scores.astype(BF16)
    gbc_ref[:, :NSTATE] = dot(grad_bf, c_in)
    gbc_ref[:, NSTATE:] = dot(grad_bf, b_in, ((0,), (0,)))

    wide_row = lax.broadcasted_iota(jnp.int32, (WIDE, 128), 0) // HEADDIM
    wide_lane = lax.broadcasted_iota(jnp.int32, (WIDE, 128), 1)
    picks = (wide_row == wide_lane).astype(F32)
    overlap_row = jnp.broadcast_to(jnp.concatenate(overlap, axis=1), (8, WIDE))
    overlap_head = dot(overlap_row, picks, precision=lax.Precision.HIGHEST)
    small_ref[...] = overlap_head
    lane8 = lax.broadcasted_iota(jnp.int32, (8, 128), 1)
    skip_row = jnp.zeros((8, 128), F32)
    for h in range(HEADS):
        skip_row = jnp.where(lane8 == h, skip_ref[h], skip_row)
    pieces = jnp.sum(grad_scores * scores, axis=0, keepdims=True)
    pieces = pieces + jnp.where(head == 0, 1.0, 0.0) * mask * base_ref[...]
    own = pieces[:, :128] + pieces[:, 128:] + (overlap_head * skip_row)[0:1]

    one, two, three = sequence_starts(stretch_ref)
    my_seq = (
        (index >= one).astype(jnp.int32)
        + (index >= two).astype(jnp.int32)
        + (index >= three).astype(jnp.int32)
    )
    own_ref[...] = jnp.where(lax.broadcasted_iota(jnp.int32, (8, 128), 0) == my_seq, own, 0.0)
    block = lax.broadcasted_iota(jnp.int32, (NCTX, 128), 0)
    lane64 = lax.broadcasted_iota(jnp.int32, (NCTX, 128), 1)
    decs = jnp.concatenate(
        [dec_ref[b // 16, (b // 2) % 8, b % 2] for b in range(NCTX)], axis=0
    )
    mine = jnp.sum(jnp.where(lane64 == index // 8, decs, 0.0), axis=1, keepdims=True)
    tab_ref[0] = jnp.broadcast_to(jnp.exp(mine), (NCTX, 128))
    begins = (block == 0) | (block == one) | (block == two) | (block == three)
    tab_ref[1] = jnp.where(begins, 0.0, 1.0)
    final = (block == NCTX - 1) | (block == one - 1) | (block == two - 1) | (block == three - 1)
    tab_ref[2] = jnp.where(final, 0.0, 1.0)
    seq = (
        (block >= one).astype(jnp.int32)
        + (block >= two).astype(jnp.int32)
        + (block >= three).astype(jnp.int32)
    )
    for j in range(4):
        tab_ref[3 + j] = jnp.where(seq == j, 1.0, 0.0)


def local_part(bc, x_act, logp_dir, step_size, mask, base, dec, rate, skip, stretches):
    vmem = pl.BlockSpec(memory_space=pltpu.VMEM)
    smem = pl.BlockSpec(memory_space=pltpu.SMEM)
    shape = jax.ShapeDtypeStruct
    return pl.pallas_call(
        local_kernel,
        name="local_part",
        out_shape=(
            shape((NCTX, 16, 128), BF16),
            shape((7, NCTX, 128), F32),
            shape((8, 128), F32),
            shape((TOK, COLS), F32),
            shape((TOK, WIDE), F32),
            shape((24, TOK), F32),
            shape((TOK, 128), F32),
            shape((TOK, WIDE), BF16),
            shape((TOK, WIDE), BF16),
            shape((8, 128), F32),
        ),
        in_specs=[vmem] * 7 + [smem] * 3,
        out_specs=tuple([vmem] * 10),
        scratch_shapes=[pltpu.VMEM((128, TOK), F32), pltpu.VMEM((8, TOK), F32)],
        compiler_params=pltpu.CompilerParams(vmem_limit_bytes=VMEM_LIMIT),
    )(bc, x_act, logp_dir, step_size, mask, base, dec, rate, skip, stretches)


def scan_kernel(
    msg_ref, tab_ref, own_ref, out_ref, sums_ref,
    got, wide, swept, reply, part, near, far, across, send_sem, recv_sem, ss, rs,
):
    index = lax.axis_index("ctx")
    x, z, c, head = place()
    barrier = pltpu.get_barrier_semaphore()

    def hello(k, carry):
        pl.semaphore_signal(
            barrier, inc=1, device_id=((index + k) % NCTX, head), device_id_type=MESH
        )
        return carry

    def hello_head(k, carry):
        pl.semaphore_signal(
            barrier, inc=1, device_id=(index, (head + k) % NHEAD), device_id_type=MESH
        )
        return carry

    lax.fori_loop(1, NCTX, hello, 0)
    lax.fori_loop(1, NHEAD, hello_head, 0)
    pl.semaphore_wait(barrier, NCTX - 1 + NHEAD - 1)

    def exchange(source, target, phase):
        def start(k, carry):
            to = (index + k) % NCTX
            pltpu.make_async_remote_copy(
                source.at[to],
                target.at[index],
                send_sem.at[phase],
                recv_sem.at[phase],
                device_id=(to, head),
                device_id_type=MESH,
            ).start()
            return carry

        lax.fori_loop(1, NCTX, start, 0)

    def settle(target, sem):
        rest = target.at[pl.ds(0, NCTX - 1)]
        pltpu.make_async_copy(rest, rest, sem).wait()

    exchange(msg_ref, got, 0)
    got[index] = msg_ref[index]
    settle(got, recv_sem.at[0])
    wide[...] = got[...].astype(F32)

    def step(b, carry):
        state, grad = carry
        r = NCTX - 1 - b
        state = state * tab_ref[1, pl.ds(b, 1)]
        grad = grad * tab_ref[2, pl.ds(r, 1)]
        swept[b, 0:8] = state
        swept[r, 8:16] = grad
        state = state * tab_ref[0, pl.ds(b, 1)] + wide[b, 0:8]
        grad = grad * tab_ref[0, pl.ds(r, 1)] + wide[r, 8:16]
        return state, grad

    zero = jnp.zeros((8, 128), F32)
    lax.fori_loop(0, NCTX, step, (zero, zero))
    reply[...] = swept[...].astype(BF16)
    exchange(reply, out_ref, 1)
    out_ref[index] = reply[index]

    met = jnp.sum(swept[:, 0:8] * wide[:, 8:16], axis=1)
    row = lax.broadcasted_iota(jnp.int32, (8, 128), 0)
    total = own_ref[...]
    for j in range(4):
        total = total + jnp.where(
            row == j, jnp.sum(met * tab_ref[3 + j], axis=0, keepdims=True), 0.0
        )
    part[0] = total

    started = []

    def share(source, target, k, partner):
        copy = pltpu.make_async_remote_copy(
            source, target, ss.at[k], rs.at[k], device_id=partner, device_id_type=MESH
        )
        copy.start()
        started.append(copy)
        return copy

    copies = []
    for k in range(1, 16):
        to = (index // 16) * 16 + (index + k) % 16
        copies.append(share(part.at[0], near.at[k - 1], k - 1, (to, head)))
    for copy in copies:
        copy.wait_recv()
    part[1] = part[0] + jnp.sum(near[...], axis=0)
    copies = []
    for k in range(1, NX):
        copies.append(share(part.at[1], far.at[k - 1], 14 + k, at(x + k, z, c, head)))
    for copy in copies:
        copy.wait_recv()
    part[2] = part[1] + jnp.sum(far[...], axis=0)
    copies = []
    for k in range(1, NHEAD):
        copies.append(share(part.at[2], across.at[k - 1], 17 + k, (index, (head + k) % NHEAD)))
    for copy in copies:
        copy.wait_recv()
    sums_ref[...] = part[2] + jnp.sum(across[...], axis=0)
    for copy in started:
        copy.wait_send()
    settle(msg_ref, send_sem.at[0])
    settle(reply, send_sem.at[1])
    settle(out_ref, recv_sem.at[1])


def scan_part(msg, tab, own):
    vmem = pl.BlockSpec(memory_space=pltpu.VMEM)
    shape = jax.ShapeDtypeStruct
    return pl.pallas_call(
        scan_kernel,
        name="scan_part",
        out_shape=(shape((NCTX, 16, 128), BF16), shape((8, 128), F32)),
        in_specs=[vmem] * 3,
        out_specs=(vmem, vmem),
        scratch_shapes=[
            pltpu.VMEM((NCTX, 16, 128), BF16),
            pltpu.VMEM((NCTX, 16, 128), F32),
            pltpu.VMEM((NCTX, 16, 128), F32),
            pltpu.VMEM((NCTX, 16, 128), BF16),
            pltpu.VMEM((3, 8, 128), F32),
            pltpu.VMEM((15, 8, 128), F32),
            pltpu.VMEM((NX - 1, 8, 128), F32),
            pltpu.VMEM((NHEAD - 1, 8, 128), F32),
            pltpu.SemaphoreType.DMA((2,)),
            pltpu.SemaphoreType.DMA((2,)),
            pltpu.SemaphoreType.DMA((25,)),
            pltpu.SemaphoreType.DMA((25,)),
        ],
        compiler_params=pltpu.CompilerParams(
            collective_id=1, has_side_effects=True, vmem_limit_bytes=VMEM_LIMIT
        ),
    )(msg, tab, own)


def halves(value):
    top = value.astype(BF16)
    return top, (value - top.astype(F32)).astype(BF16)


def grad_kernel(
    states_ref, sums_ref, bc_ref, x_ref, xf_ref, dyg_ref, gbc_ref, gx_ref, rows_ref, cols_ref, small_ref,
    step_ref, rate_ref, stretch_ref,
    grad_x_ref, grad_step_ref, grad_cols_ref, few_ref,
):
    index = lax.axis_index("ctx")
    one, two, three = sequence_starts(stretch_ref)
    seq_sums = jnp.sum(sums_ref[...], axis=1, keepdims=True)
    first = seq_sums[0:1] - seq_sums[1:2]
    second = seq_sums[2:3] - seq_sums[3:4]
    margin = jnp.where(index >= two, second, first)
    coef = 1.0 / (1.0 + jnp.exp(-hinge_sharp * (hinge_margin - margin)))
    rejected = ((index >= one) & (index < two)) | (index >= three)
    scale = jnp.where(rejected, coef, -coef)

    states = states_ref[...].astype(F32)
    state_in = states[:, 0:8].reshape(WIDE, NSTATE)
    grad_state = states[:, 8:16].reshape(WIDE, NSTATE)
    state_bf, grad_bf = state_in.astype(BF16), grad_state.astype(BF16)
    bc = bc_ref[...]
    b_in, c_in = bc[:, :NSTATE], bc[:, NSTATE:]
    columns = cols_ref[...]
    low_half = lax.broadcasted_iota(jnp.int32, (TOK, 128), 1) < HEADDIM
    pick_row = lax.broadcasted_iota(jnp.int32, (8, 128), 0)
    pick_half = lax.broadcasted_iota(jnp.int32, (8, 128), 1) // HEADDIM
    nt = ((1,), (1,))
    carried = jnp.zeros((8, TOK), F32)
    kept = jnp.zeros((8, TOK), F32)
    for pair in range(HEADS // 2):
        span = slice(128 * pair, 128 * pair + 128)
        picks = (pick_row == 2 * pair + pick_half).astype(BF16)
        left = dot(c_in, state_bf[span], nt) * dyg_ref[:, span].astype(F32)
        top, low = halves(left)
        carried = carried + dot(picks, top, nt) + dot(picks, low, nt)
        back = dot(b_in, grad_bf[span], nt) * pair_columns(columns, 16, pair, low_half)
        top, low = halves(back * x_ref[:, span].astype(F32))
        kept = kept + dot(picks, top, nt) + dot(picks, low, nt)
        grad_x_ref[:, span] = ((gx_ref[:, span] + back) * scale).astype(BF16)
    grad_b = gbc_ref[:, :NSTATE] + dot(xf_ref[...], grad_bf)
    grad_c = gbc_ref[:, NSTATE:] + dot(dyg_ref[...], state_bf)
    grad_cols_ref[:, :NSTATE] = (grad_b * scale).astype(BF16)
    grad_cols_ref[:, NSTATE:] = (grad_c * scale).astype(BF16)

    cum, drow, dcol = rows_ref[0:8], rows_ref[8:16], rows_ref[16:24]
    step = step_ref[...]
    row8 = lax.broadcasted_iota(jnp.int32, (8, TOK), 0)
    rate = jnp.zeros((8, TOK), F32)
    for h in range(HEADS):
        rate = jnp.where(row8 == h, rate_ref[h], rate)
    grad_decay = jnp.sum(
        jnp.sum((state_in * grad_state).reshape(HEADS, HEADDIM, NSTATE), axis=1), axis=1, keepdims=True
    )
    end = jnp.sum(kept, axis=1, keepdims=True) + grad_decay * jnp.exp(cum[:, TOK - 1 : TOK])
    token = lax.broadcasted_iota(jnp.int32, (8, TOK), 1)
    grad_cum = drow - dcol + carried - kept + jnp.where(token == TOK - 1, end, 0.0)
    t_index = lax.broadcasted_iota(jnp.int32, (TOK, TOK), 0)
    u_index = lax.broadcasted_iota(jnp.int32, (TOK, TOK), 1)
    tail = dot(grad_cum, (t_index >= u_index).astype(F32), precision=lax.Precision.HIGHEST)
    grad_step_ref[...] = ((dcol + kept) / step - rate * tail) * scale
    grad_rate = -jnp.sum(step * tail, axis=1, keepdims=True)
    lane = lax.broadcasted_iota(jnp.int32, (8, 128), 1)
    rate_row = jnp.sum(jnp.where(lane == pick_row, grad_rate, 0.0), axis=0, keepdims=True)
    few_ref[...] = jnp.where(pick_row == 0, rate_row, small_ref[...]) * scale


def grad_part(states, sums, bc, x_act, xf, dyg, gbc, gx, rows, cols, small, step_size, rate, stretches):
    vmem = pl.BlockSpec(memory_space=pltpu.VMEM)
    smem = pl.BlockSpec(memory_space=pltpu.SMEM)
    shape = jax.ShapeDtypeStruct
    return pl.pallas_call(
        grad_kernel,
        name="grad_part",
        out_shape=(
            shape((TOK, WIDE), BF16),
            shape((8, TOK), F32),
            shape((TOK, COLS), BF16),
            shape((8, 128), F32),
        ),
        in_specs=[vmem] * 12 + [smem] * 2,
        out_specs=tuple([vmem] * 4),
        compiler_params=pltpu.CompilerParams(vmem_limit_bytes=VMEM_LIMIT),
    )(states, sums, bc, x_act, xf, dyg, gbc, gx, rows, cols, small, step_size, rate, stretches)


def reduce_kernel(
    hid_ref, cols_ref, few_ref, out_ref, total_ref,
    hid, prod, mate_out, mate_in, a_out, a_own, a_in, a2_out, a2_own, a2_in,
    b_out, b_own, b_in, b2_out, b2_own, b2_in, few, few_c, few_z, few_x, load_sem, ss, rs,
):
    x, z, c, head = place()
    load = pltpu.make_async_copy(hid_ref, hid, load_sem)
    load.start()
    greet(plane_partners(x, z, c, head))
    mate = at(x, z, 1 - c, head)
    started = []

    def send(source, target, k, partner):
        copy = pltpu.make_async_remote_copy(
            source, target, ss.at[k], rs.at[k], device_id=partner, device_id_type=MESH
        )
        copy.start()
        started.append(copy)
        return copy

    few[0] = few_ref[...]
    few_copy = send(few.at[0], few_c, 0, mate)
    load.wait()
    grads = cols_ref[...]
    span = MODEL // NX
    order = (2, 1, 3, 0)
    mate_copies = {}
    for dx in order:
        to = (x + dx) % NX
        chunk = hid[:, pl.ds(pl.multiple_of(to * span, span), span)]
        prod[dx] = dot(chunk, grads, ((0,), (0,))).reshape(NZ, NC, DEPTH, COLS)
        mate_out[dx] = prod[dx, :, 1 - c].astype(BF16)
        mate_copies[dx] = send(mate_out.at[dx], mate_in.at[dx], 1 + dx, mate)
    few_copy.wait_recv()
    few[1] = few[0] + few_c[...]
    few_copies = [
        send(few.at[1], few_z.at[dz - 1], 4 + dz, at(x, z + dz, c, head)) for dz in range(1, NZ)
    ]
    a_copies = []
    for dx in order:
        mate_copies[dx].wait_recv()
        chip = prod[dx, :, c] + mate_in[dx].astype(F32)
        b_own[dx] = chip[:, PART:]
        b_out[:, dx] = chip[:, PART:].astype(BF16)
        if dx:
            a_out[dx - 1] = chip[:, :PART].astype(BF16)
            a_copies.append(send(a_out.at[dx - 1], a_in.at[dx - 1], 11 + dx, at(x + dx, z, c, head)))
        else:
            a_own[...] = chip[:, :PART]
    b_copies = [
        send(b_out.at[(z + dz) % NZ], b_in.at[dz - 1], 14 + dz, at(x, z + dz, c, head))
        for dz in (4, 3, 5, 2, 6, 1, 7)
    ]
    for copy in few_copies:
        copy.wait_recv()
    few[2] = few[1] + jnp.sum(few_z[...], axis=0)
    few_copies = [
        send(few.at[2], few_x.at[dx - 1], 21 + dx, at(x + dx, z, c, head)) for dx in range(1, NX)
    ]
    for copy in b_copies:
        copy.wait_recv()
    b2_own[...] = b_own[:, z] + jnp.sum(b_in[...].astype(F32), axis=0)
    b2_out[...] = b2_own[...].astype(BF16)
    b2_copies = [
        send(b2_out.at[dx], b2_in.at[dx - 1], 24 + dx, at(x + dx, z, c, head)) for dx in range(1, NX)
    ]
    for copy in a_copies:
        copy.wait_recv()
    a2_own[...] = a_own[...] + jnp.sum(a_in[...].astype(F32), axis=0)
    a2_out[...] = a2_own[...].astype(BF16)
    a2_copies = [
        send(a2_out.at[(z + dz) % NZ], a2_in.at[dz - 1], 27 + dz, at(x, z + dz, c, head))
        for dz in (4, 3, 5, 2, 6, 1, 7)
    ]
    for copy in few_copies + b2_copies:
        copy.wait_recv()
    total_ref[...] = few[2] + jnp.sum(few_x[...], axis=0)
    out_ref[PART:] = b2_own[0] + jnp.sum(b2_in[...].astype(F32), axis=0)
    for copy in a2_copies:
        copy.wait_recv()
    out_ref[:PART] = a2_own[z] + jnp.sum(a2_in[...].astype(F32), axis=0)
    for copy in started:
        copy.wait_send()


def reduce_part(hidden, grad_cols, few):
    vmem = pl.BlockSpec(memory_space=pltpu.VMEM)
    shape = jax.ShapeDtypeStruct
    rest = DEPTH - PART
    return pl.pallas_call(
        reduce_kernel,
        name="reduce_part",
        out_shape=(shape((DEPTH, COLS), F32), shape((8, 128), F32)),
        in_specs=[pl.BlockSpec(memory_space=pl.ANY), vmem, vmem],
        out_specs=(vmem, vmem),
        scratch_shapes=[
            pltpu.VMEM((TOK, MODEL), BF16),
            pltpu.VMEM((NX, NZ, NC, DEPTH, COLS), F32),
            pltpu.VMEM((NX, NZ, DEPTH, COLS), BF16),
            pltpu.VMEM((NX, NZ, DEPTH, COLS), BF16),
            pltpu.VMEM((NX - 1, NZ, PART, COLS), BF16),
            pltpu.VMEM((NZ, PART, COLS), F32),
            pltpu.VMEM((NX - 1, NZ, PART, COLS), BF16),
            pltpu.VMEM((NZ, PART, COLS), BF16),
            pltpu.VMEM((NZ, PART, COLS), F32),
            pltpu.VMEM((NZ - 1, PART, COLS), BF16),
            pltpu.VMEM((NZ, NX, rest, COLS), BF16),
            pltpu.VMEM((NX, NZ, rest, COLS), F32),
            pltpu.VMEM((NZ - 1, NX, rest, COLS), BF16),
            pltpu.VMEM((NX, rest, COLS), BF16),
            pltpu.VMEM((NX, rest, COLS), F32),
            pltpu.VMEM((NX - 1, rest, COLS), BF16),
            pltpu.VMEM((3, 8, 128), F32),
            pltpu.VMEM((8, 128), F32),
            pltpu.VMEM((NZ - 1, 8, 128), F32),
            pltpu.VMEM((NX - 1, 8, 128), F32),
            pltpu.SemaphoreType.DMA,
            pltpu.SemaphoreType.DMA((35,)),
            pltpu.SemaphoreType.DMA((35,)),
        ],
        compiler_params=pltpu.CompilerParams(
            collective_id=2, has_side_effects=True, vmem_limit_bytes=VMEM_LIMIT
        ),
    )(hidden, grad_cols, few)


def body(
    hidden, w_bc, x_act, step_size, decay_rate, skip_gain, logp_dir, base_logp, seq_stretches, resp_mask
):
    bc, dec = gather(w_bc, step_size, decay_rate, hidden)
    msg, tab, own, gbc, gx, rows, cols, xf, dyg, small = local_part(
        bc, x_act, logp_dir, step_size, resp_mask.reshape(1, TOK), base_logp.reshape(1, TOK), dec,
        decay_rate, skip_gain, seq_stretches,
    )
    states, sums = scan_part(msg, tab, own)
    grad_x, grad_step, grad_cols, few = grad_part(
        states, sums, bc, x_act, xf, dyg, gbc, gx, rows, cols, small, step_size, decay_rate, seq_stretches
    )
    grad_w, total = reduce_part(hidden, grad_cols, few)
    return grad_x, grad_step, total[0, :HEADS], total[1, :HEADS], grad_w


def solution(mesh):
    return jax.shard_map(
        body,
        mesh=mesh,
        in_specs=(
            P("ctx", None),
            P("ctx", "head"),
            P("ctx", "head"),
            P("head", "ctx"),
            P("head"),
            P("head"),
            P("ctx", "head"),
            P("ctx"),
            P(),
            P("ctx"),
        ),
        out_specs=(P("ctx", "head"), P("head", "ctx"), P("head"), P("head"), P("ctx", "head")),
        check_vma=False,
    )
```

```python
import functools

import jax
import jax.numpy as jnp
from jax import lax
from jax.experimental import pallas as pl
from jax.experimental.pallas import tpu as pltpu
from jax.sharding import PartitionSpec as P

HEADDIM = 64
NSTATE = 128
NX, NZ, NC = 4, 8, 2
NCTX = NX * NZ * NC
CHIPS = NX * NZ
NHEAD = 8
TOK = 256
HEADS = 8
WIDE = HEADS * HEADDIM
DEPTH = 64
COLS = 2 * NSTATE
MODEL = NCTX * DEPTH
PART = 48

hinge_sharp = 0.005
hinge_margin = 10.0

MESH = pl.DeviceIdType.MESH
F32 = jnp.float32
BF16 = jnp.bfloat16
VMEM_LIMIT = 48 << 20
SPACE = pltpu.HBM


def place():
    index = lax.axis_index("ctx")
    return index // 16, (index // 2) % 8, index % 2, lax.axis_index("head")


def at(x, z, c, head):
    return (((x % NX) * NZ + (z % NZ)) * NC + c, head)


def greet(partners):
    barrier = pltpu.get_barrier_semaphore()
    for partner in partners:
        pl.semaphore_signal(barrier, inc=1, device_id=partner, device_id_type=MESH)
    pl.semaphore_wait(barrier, len(partners))


def plane_partners(x, z, c, head):
    return (
        [at(x, z + dz, c, head) for dz in range(1, NZ)]
        + [at(x + dx, z, c, head) for dx in range(1, NX)]
        + [at(x, z, 1 - c, head)]
    )


def dot(left, right, dims=((1,), (0,)), precision=None):
    return lax.dot_general(left, right, (dims, ((), ())), precision=precision, preferred_element_type=F32)


def pair_columns(columns, base, pair, low_half):
    one, two = base + 2 * pair, base + 2 * pair + 1
    return jnp.where(low_half, columns[:, one : one + 1], columns[:, two : two + 1])


def sequence_starts(stretch_ref):
    one = stretch_ref[0]
    two = one + stretch_ref[1]
    return one, two, two + stretch_ref[2]


def halves(value):
    top = value.astype(BF16)
    return top, (value - top.astype(F32)).astype(BF16)


def keep_of(block, starts):
    begins = block == 0
    for start in starts:
        begins = begins | (block == start)
    return jnp.where(begins, 0.0, 1.0)


def seq_of(block, starts):
    return sum((block >= start).astype(jnp.int32) for start in starts)


def front_kernel(
    hid_hbm, w_hbm, x_hbm, dir_hbm, step_hbm, rate_hbm, skip_hbm, mask_hbm, base_hbm, stretch_hbm,
    gx_ref, gstep_ref, gcols_ref, few_ref, sums_ref,
    hid, x_ref, dir_ref, step_ref, rate_ref, skip_ref, mask_ref, base_ref, stretch_ref,
    buf, dec, factors, moves, stack, cols_ref, xf_ref, dyg_ref, drow, dcol, lg, mate_lg, msg, got, wide,
    swept, reply, states, tab, part, near, across,
    load_sem, send_sem, recv_sem, ss, rs, gs, gr,
):
    index = lax.axis_index("ctx")
    x, z, c, head = place()
    chip = index // 2
    mate = at(x, z, 1 - c, head)
    every = slice(None)

    loads = {}
    for k, (name, source, target) in enumerate(
        (
            ("step", step_hbm, step_ref),
            ("rate", rate_hbm, rate_ref),
            ("w", w_hbm, buf.at[x, z, c]),
            ("mask", mask_hbm, mask_ref),
            ("x", x_hbm, x_ref),
            ("dir", dir_hbm, dir_ref),
            ("skip", skip_hbm, skip_ref),
            ("base", base_hbm, base_ref),
            ("stretch", stretch_hbm, stretch_ref),
            ("hid", hid_hbm, hid),
        )
    ):
        loads[name] = pltpu.make_async_copy(source, target, load_sem.at[k])
        loads[name].start()

    barrier = pltpu.get_barrier_semaphore()

    def hello(k, carry):
        to = (chip + k) % CHIPS
        pl.semaphore_signal(barrier, inc=1, device_id=(to * 2 + c, head), device_id_type=MESH)
        return carry

    def hello_head(k, carry):
        to = (head + k // 2) % NHEAD
        who = chip * 2 + (c + k) % 2
        pl.semaphore_signal(barrier, inc=1, device_id=(who, to), device_id_type=MESH)
        return carry

    lax.fori_loop(1, CHIPS, hello, 0)
    lax.fori_loop(1, 2 * NHEAD, hello_head, 0)
    loads["w"].wait()
    pl.semaphore_wait(barrier, CHIPS - 1 + 2 * NHEAD - 1)

    started, slots = [], {}

    def slot(key):
        return slots.setdefault(key, len(slots))

    def send(ref, where, key, partner, into=None):
        k = slot(key)
        copy = pltpu.make_async_remote_copy(
            ref.at[where],
            (ref if into is None else into).at[where],
            ss.at[k],
            rs.at[k],
            device_id=partner,
            device_id_type=MESH,
        )
        copy.start()
        started.append(copy)

    def arrive(ref, where, key):
        piece = ref.at[where]
        k = slot(key)
        pltpu.make_async_remote_copy(
            piece, piece, ss.at[k], rs.at[k], device_id=mate, device_id_type=MESH
        ).wait_recv()

    low, high = pl.ds(0, PART), pl.ds(PART, DEPTH - PART)
    near_z, near_x = (1, 7, 2, 6, 3, 5, 4), (1, 3, 2)

    def to_z(dz):
        return at(x, z + dz, c, head)

    def to_x(dx):
        return at(x + dx, z, c, head)

    def from_z(dz):
        return (z - dz) % NZ

    def from_x(dx):
        return (x - dx) % NX

    for dz in near_z:
        send(buf, (x, z, c, low), ("az", dz), to_z(dz))
    for dx in near_x:
        send(buf, (x, z, c, high), ("bx", dx), to_x(dx))
    for dx in near_x:
        send(buf, (x, z, c, low), ("ax", 0, dx), to_x(dx))
    for dz in near_z:
        send(buf, (x, z, c, high), ("bz", 0, dz), to_z(dz))
    send(buf, (x, z, c), ("own",), mate)

    loads["step"].wait()
    loads["rate"].wait()
    rows8 = lax.broadcasted_iota(jnp.int32, (8, 128), 0)
    lanes8 = lax.broadcasted_iota(jnp.int32, (8, 128), 1)
    step = step_ref[...]
    row8 = lax.broadcasted_iota(jnp.int32, (8, TOK), 0)
    rate = jnp.zeros((8, TOK), F32)
    for h in range(HEADS):
        rate = jnp.where(row8 == h, rate_ref[h], rate)
    total = -rate[:, 0:1] * jnp.sum(step, axis=1, keepdims=True)
    dec[x, z, c] = jnp.sum(jnp.where(rows8 == lanes8, total, 0.0), axis=0, keepdims=True)
    for dz in near_z:
        send(dec, (x, z, c), ("dz", dz), to_z(dz))

    s_index = lax.broadcasted_iota(jnp.int32, (TOK, TOK), 0)
    t_index = lax.broadcasted_iota(jnp.int32, (TOK, TOK), 1)
    causal = s_index <= t_index
    cum = -rate * dot(step, causal.astype(F32), precision=lax.Precision.HIGHEST)
    last = cum[:, TOK - 1 : TOK]
    loads["mask"].wait()
    mask = mask_ref[...].astype(F32)
    stack[...] = jnp.zeros((128, TOK), F32)
    stack[0:8] = cum - jnp.log(step)
    stack[8:16] = jnp.exp(cum)
    stack[16:24] = jnp.exp(last - cum) * step
    stack[24:32] = jnp.broadcast_to(mask, (8, TOK))
    columns = stack[...].T
    cols_ref[...] = columns
    loads["x"].wait()
    loads["dir"].wait()
    loads["skip"].wait()
    loads["base"].wait()
    loads["stretch"].wait()
    low_half = lax.broadcasted_iota(jnp.int32, (TOK, 128), 1) < HEADDIM
    overlap = []

    def prepare(pair):
        columns = cols_ref[...]
        span = slice(128 * pair, 128 * pair + 128)
        x_pair = x_ref[:, span]
        x_wide = x_pair.astype(F32)
        dy_wide = dir_ref[:, span].astype(F32) * columns[:, 24:25]
        dy_pair = dy_wide.astype(BF16)
        dir_ref[:, span] = dy_pair
        xf_ref[:, span] = (x_wide * pair_columns(columns, 16, pair, low_half)).astype(BF16)
        dyg_ref[:, span] = (dy_wide * pair_columns(columns, 8, pair, low_half)).astype(BF16)
        overlap.append(jnp.sum(x_wide * dy_wide, axis=0, keepdims=True))
        for h in (2 * pair, 2 * pair + 1):
            half = slice(HEADDIM * (h % 2), HEADDIM * (h % 2) + HEADDIM)
            gap = jnp.where(causal, cum[h : h + 1, :] - columns[:, h : h + 1], -1e30)
            factor = jnp.exp(gap)
            factors[h] = factor
            moves[h] = dot(x_pair[:, half], dy_pair[:, half], ((1,), (1,))) * factor
        skip_pair = jnp.where(low_half, skip_ref[2 * pair], skip_ref[2 * pair + 1])
        gx_ref[:, span] = skip_pair * dy_wide

    def forward_low(dz):
        where = (x, from_z(dz), c, low)
        arrive(buf, where, ("az", dz))
        for dx in near_x:
            send(buf, where, ("ax", dz, dx), to_x(dx))
        send(buf, where, ("am", dz), mate)

    def forward_high(dx):
        where = (from_x(dx), z, c, high)
        arrive(buf, where, ("bx", dx))
        for dz in near_z:
            send(buf, where, ("bz", dx, dz), to_z(dz))
        send(buf, where, ("bm", dx), mate)

    def take_low(dz, dx):
        where = (from_x(dx), from_z(dz), c, low)
        arrive(buf, where, ("ax", dz, dx))
        send(buf, where, ("axm", dz, dx), mate)

    def take_high(dz):
        for dx in (0, 1, 3, 2):
            arrive(buf, (from_x(dx), from_z(dz), c, high), ("bz", dx, dz))
        send(buf, (every, from_z(dz), c, high), ("bzm", dz), mate)

    prepare(0)
    for dz in (1, 7):
        forward_low(dz)
    for dx in (1, 3):
        forward_high(dx)
    prepare(1)
    for dz in (2, 6):
        forward_low(dz)
    forward_high(2)
    prepare(2)
    for dz in (3, 5, 4):
        forward_low(dz)
    for dz in near_z:
        arrive(dec, (x, from_z(dz), c), ("dz", dz))
    for dx in near_x:
        send(dec, (x, every, c), ("dx", dx), to_x(dx))
    prepare(3)
    for dx in near_x:
        take_low(0, dx)
    for dz in (1, 7):
        for dx in near_x:
            take_low(dz, dx)
    for dz in (1, 7):
        take_high(dz)
    for dz in (2, 6):
        for dx in near_x:
            take_low(dz, dx)
    for dz in (2, 6):
        take_high(dz)
    for dx in near_x:
        arrive(dec, (from_x(dx), every, c), ("dx", dx))
    send(dec, (every, every, c), ("dm",), mate)
    for dz in (3, 5, 4):
        for dx in near_x:
            take_low(dz, dx)
        take_high(dz)

    other = 1 - c
    arrive(buf, (x, z, other), ("own",))
    for dz in near_z:
        arrive(buf, (x, from_z(dz), other, low), ("am", dz))
    for dx in near_x:
        arrive(buf, (from_x(dx), z, other, high), ("bm", dx))
    for dz in (0,) + near_z:
        for dx in near_x:
            arrive(buf, (from_x(dx), from_z(dz), other, low), ("axm", dz, dx))
    for dz in near_z:
        arrive(buf, (every, from_z(dz), other, high), ("bzm", dz))
    loads["hid"].wait()
    span = MODEL // NX
    sums = jnp.zeros((TOK, COLS), F32)
    for k in range(NX):
        sums = sums + dot(hid[:, k * span : (k + 1) * span], buf[k].reshape(span, COLS))
    bc = sums.astype(BF16)
    b_in, c_in = bc[:, :NSTATE], bc[:, NSTATE:]
    lg[0] = dot(xf_ref[...], b_in, ((0,), (0,))).reshape(2, WIDE // 2, NSTATE)
    lg[1] = dot(dyg_ref[...], c_in, ((0,), (0,))).reshape(2, WIDE // 2, NSTATE)
    send(lg, (every, other), ("l1",), mate, mate_lg)
    send(lg, (every, c), ("l2",), mate, mate_lg)

    starts = sequence_starts(stretch_ref)
    arrive(dec, (every, every, other), ("dm",))
    row0, row1 = jnp.exp(dec[x, z, 0]), jnp.exp(dec[x, z, 1])
    lane1 = lax.broadcasted_iota(jnp.int32, (1, 128), 1)

    def pick(row, h):
        return jnp.sum(jnp.where(lane1 == h, row, 0.0), axis=1, keepdims=True)

    keep0, keep1 = keep_of(2 * chip, starts), keep_of(2 * chip + 1, starts)
    next1 = jnp.where(2 * chip + 2 == NCTX, 0.0, keep_of(2 * chip + 2, starts))
    first = c == 0
    arrive(mate_lg, (every, c), ("l1",))
    met = jnp.zeros((HEADDIM, 128), F32)
    chip_l, chip_g = [], []
    for hh in range(HEADS // 2):
        span = slice(HEADDIM * hh, HEADDIM * hh + HEADDIM)
        mine_l, mine_g = lg[0, c, span], lg[1, c, span]
        mate_l, mate_g = mate_lg[0, c, span], mate_lg[1, c, span]
        l0, l1 = jnp.where(first, mine_l, mate_l), jnp.where(first, mate_l, mine_l)
        g0, g1 = jnp.where(first, mine_g, mate_g), jnp.where(first, mate_g, mine_g)
        h = 4 * c + hh
        chip_l.append(pick(row1, h) * keep1 * l0 + l1)
        chip_g.append(pick(row0, h) * keep1 * g1 + g0)
        met = met + l0 * g1
    msg[...] = jnp.concatenate(
        [
            jnp.concatenate(chip_l, axis=0).reshape(CHIPS, 8, 128),
            jnp.concatenate(chip_g, axis=0).reshape(CHIPS, 8, 128),
        ],
        axis=1,
    ).astype(BF16)

    def exchange(source, target, phase):
        def start(k, carry):
            to = (chip + k) % CHIPS
            pltpu.make_async_remote_copy(
                source.at[to],
                target.at[chip],
                send_sem.at[phase],
                recv_sem.at[phase],
                device_id=(to * 2 + c, head),
                device_id_type=MESH,
            ).start()
            return carry

        lax.fori_loop(1, CHIPS, start, 0)

    def settle(target, sem):
        rest = target.at[pl.ds(0, CHIPS - 1)]
        pltpu.make_async_copy(rest, rest, sem).wait()

    exchange(msg, got, 0)
    got[chip] = msg[chip]

    scores = dot(b_in, c_in, ((1,), (1,)))
    grad_scores = jnp.zeros((TOK, TOK), F32)
    back = jnp.zeros((TOK, 128), F32)
    lane128 = lax.broadcasted_iota(jnp.int32, (TOK, 128), 1)
    for pair in range(HEADS // 2):
        span = slice(128 * pair, 128 * pair + 128)
        within = []
        for h in (2 * pair, 2 * pair + 1):
            moved = moves[h]
            grad_scores = grad_scores + moved
            spent = moved * scores
            drow[h : h + 1] = jnp.sum(spent, axis=0, keepdims=True)
            back = jnp.where(lane128 == h, jnp.sum(spent, axis=1, keepdims=True), back)
            dy_h = dir_ref[:, HEADDIM * h : HEADDIM * h + HEADDIM]
            within.append(dot((scores * factors[h]).astype(BF16), dy_h))
        gx_ref[:, span] = gx_ref[:, span] + jnp.concatenate(within, axis=1)
    dcol[...] = back.T[0:8]
    grad_bf = grad_scores.astype(BF16)
    gcols_ref[:, :NSTATE] = dot(grad_bf, c_in)
    gcols_ref[:, NSTATE:] = dot(grad_bf, b_in, ((0,), (0,)))

    wide_row = lax.broadcasted_iota(jnp.int32, (WIDE, 128), 0) // HEADDIM
    wide_lane = lax.broadcasted_iota(jnp.int32, (WIDE, 128), 1)
    overlap_row = jnp.broadcast_to(jnp.concatenate(overlap, axis=1), (8, WIDE))
    overlap_head = dot(overlap_row, (wide_row == wide_lane).astype(F32), precision=lax.Precision.HIGHEST)
    few_ref[...] = overlap_head
    skip_row = jnp.zeros((1, 128), F32)
    for h in range(HEADS):
        skip_row = jnp.where(lane1 == h, skip_ref[h], skip_row)
    pieces = jnp.sum(grad_scores * scores, axis=0, keepdims=True)
    pieces = pieces + jnp.where(head == 0, 1.0, 0.0) * mask * base_ref[...]
    own = pieces[:, :128] + pieces[:, 128:] + overlap_head[0:1] * skip_row
    own = jnp.sum(own, axis=1, keepdims=True)
    pair_sum = keep1 * jnp.sum(jnp.sum(met, axis=0, keepdims=True), axis=1, keepdims=True)
    mine = jnp.where(lane1 == seq_of(index, starts), own, 0.0)
    mine = mine + jnp.where(lane1 == seq_of(2 * chip + 1, starts), pair_sum, 0.0)

    chips = lax.broadcasted_iota(jnp.int32, (CHIPS, 128), 0)
    lane32 = lax.broadcasted_iota(jnp.int32, (CHIPS, 128), 1)
    my_head = 4 * c + chip // 8

    def decays(core):
        table = jnp.concatenate([dec[m // NZ, m % NZ, core] for m in range(CHIPS)], axis=0)
        return jnp.exp(jnp.sum(jnp.where(lane32 == my_head, table, 0.0), axis=1, keepdims=True))

    both = decays(0) * decays(1) * keep_of(2 * chips + 1, starts)
    enters = keep_of(2 * chips, starts)
    tab[0] = both * enters
    tab[1] = both * jnp.where(chips == CHIPS - 1, 0.0, keep_of(2 * chips + 2, starts))

    settle(got, recv_sem.at[0])
    wide[...] = got[...].astype(F32)

    def advance(b, carry):
        state, grad = carry
        r = CHIPS - 1 - b
        swept[b, 0:8] = state
        swept[r, 8:16] = grad
        state = state * tab[0, pl.ds(b, 1)] + wide[b, 0:8]
        grad = grad * tab[1, pl.ds(r, 1)] + wide[r, 8:16]
        return state, grad

    zero = jnp.zeros((8, 128), F32)
    lax.fori_loop(0, CHIPS, advance, (zero, zero))
    reply[...] = swept[...].astype(BF16)
    exchange(reply, states.at[c], 1)
    states[c, chip] = reply[chip]

    met = jnp.sum(swept[:, 0:8] * wide[:, 8:16], axis=1) * enters
    met = jnp.sum(met, axis=1, keepdims=True)
    seqs = seq_of(2 * chips, starts)
    mine = mine + jnp.sum(jnp.where(lane32 == seqs, met, 0.0), axis=0, keepdims=True)
    part[0] = mine

    def spread(k, carry):
        to = (chip + k) % CHIPS
        pltpu.make_async_remote_copy(
            part.at[0], near.at[k], gs.at[0], gr.at[0], device_id=(to * 2 + c, head), device_id_type=MESH
        ).start()
        return carry

    lax.fori_loop(1, CHIPS, spread, 0)
    near[0] = mine

    def settle_few(target, sem, count):
        rest = target.at[pl.ds(1, count)]
        pltpu.make_async_copy(rest, rest, sem).wait()

    settle_few(near, gr.at[0], CHIPS - 1)
    gathered = jnp.sum(near[...], axis=0)
    part[1] = gathered

    def spread_head(k, carry):
        to = (head + k // 2) % NHEAD
        who = chip * 2 + (c + k) % 2
        pltpu.make_async_remote_copy(
            part.at[1], across.at[k], gs.at[1], gr.at[1], device_id=(who, to), device_id_type=MESH
        ).start()
        return carry

    lax.fori_loop(1, 2 * NHEAD, spread_head, 0)
    across[0] = gathered

    settle(states.at[c], recv_sem.at[1])
    send(states, (c,), ("st",), mate)
    arrive(mate_lg, (every, other), ("l2",))

    def spaced(row):
        return jnp.concatenate(
            [jnp.broadcast_to(pick(row, h), (HEADDIM, 128)) for h in range(HEADS)], axis=0
        )

    lead = jnp.where(first, keep0, keep0 * keep1 * spaced(row0))
    lead_mate = jnp.where(first, 0.0, keep1)
    trail = jnp.where(first, next1 * keep1 * spaced(row1), next1)
    trail_mate = jnp.where(first, keep1, 0.0)
    arrive(states, (other,), ("st",))
    states_f = states[...].astype(F32)
    state_in = lead * states_f[:, :, 0:8].reshape(WIDE, NSTATE)
    state_in = state_in + lead_mate * mate_lg[0].reshape(WIDE, NSTATE)
    grad_state = trail * states_f[:, :, 8:16].reshape(WIDE, NSTATE)
    grad_state = grad_state + trail_mate * mate_lg[1].reshape(WIDE, NSTATE)

    columns = cols_ref[...]
    state_bf, gstate_bf = state_in.astype(BF16), grad_state.astype(BF16)
    pick_half = lanes8 // HEADDIM
    nt = ((1,), (1,))
    carried = jnp.zeros((8, TOK), F32)
    kept = jnp.zeros((8, TOK), F32)
    for pair in range(HEADS // 2):
        span = slice(128 * pair, 128 * pair + 128)
        picks = (rows8 == 2 * pair + pick_half).astype(BF16)
        top, rest = halves(dot(c_in, state_bf[span], nt) * dyg_ref[:, span].astype(F32))
        carried = carried + dot(picks, top, nt) + dot(picks, rest, nt)
        pulled = dot(b_in, gstate_bf[span], nt) * pair_columns(columns, 16, pair, low_half)
        top, rest = halves(pulled * x_ref[:, span].astype(F32))
        kept = kept + dot(picks, top, nt) + dot(picks, rest, nt)
        gx_ref[:, span] = gx_ref[:, span] + pulled
    gcols_ref[:, :NSTATE] = gcols_ref[:, :NSTATE] + dot(xf_ref[...], gstate_bf)
    gcols_ref[:, NSTATE:] = gcols_ref[:, NSTATE:] + dot(dyg_ref[...], state_bf)

    grad_decay = jnp.sum(
        jnp.sum((state_in * grad_state).reshape(HEADS, HEADDIM, NSTATE), axis=1), axis=1, keepdims=True
    )
    end = jnp.sum(kept, axis=1, keepdims=True) + grad_decay * jnp.exp(last)
    token = lax.broadcasted_iota(jnp.int32, (8, TOK), 1)
    grad_cum = drow[...] - dcol[...] + carried - kept + jnp.where(token == TOK - 1, end, 0.0)
    tail = dot(grad_cum, (s_index >= t_index).astype(F32), precision=lax.Precision.HIGHEST)
    gstep_ref[...] = (dcol[...] + kept) / step - rate * tail
    grad_rate = -jnp.sum(step * tail, axis=1, keepdims=True)
    rate_row = jnp.sum(jnp.where(lanes8 == rows8, grad_rate, 0.0), axis=0, keepdims=True)
    few_ref[...] = jnp.where(rows8 == 0, rate_row, few_ref[...])

    settle_few(across, gr.at[1], 2 * NHEAD - 1)
    sums_ref[...] = jnp.broadcast_to(jnp.sum(across[...], axis=0), (8, 128))
    for copy in started:
        copy.wait_send()
    settle(msg, send_sem.at[0])
    settle(reply, send_sem.at[1])
    settle_few(near, gs.at[0], CHIPS - 1)
    settle_few(across, gs.at[1], 2 * NHEAD - 1)


def front(hidden, w_bc, x_act, logp_dir, step_size, rate, skip, mask, base, stretches):
    shape = jax.ShapeDtypeStruct
    vmem = pl.BlockSpec(memory_space=pltpu.VMEM)
    count = 120
    return pl.pallas_call(
        front_kernel,
        name="front",
        out_shape=(
            shape((TOK, WIDE), F32),
            shape((8, TOK), F32),
            shape((TOK, COLS), F32),
            shape((8, 128), F32),
            shape((8, 128), F32),
        ),
        in_specs=[pl.BlockSpec(memory_space=SPACE)] * 10,
        out_specs=tuple([vmem] * 5),
        scratch_shapes=[
            pltpu.VMEM((TOK, MODEL), BF16),
            pltpu.VMEM((TOK, WIDE), BF16),
            pltpu.VMEM((TOK, WIDE), BF16),
            pltpu.VMEM((8, TOK), F32),
            pltpu.SMEM((8,), F32),
            pltpu.SMEM((8,), F32),
            pltpu.VMEM((1, TOK), jnp.int32),
            pltpu.VMEM((1, TOK), F32),
            pltpu.SMEM((4,), jnp.int32),
            pltpu.VMEM((NX, NZ, NC, DEPTH, COLS), BF16),
            pltpu.VMEM((NX, NZ, NC, 1, 128), F32),
            pltpu.VMEM((HEADS, TOK, TOK), F32),
            pltpu.VMEM((HEADS, TOK, TOK), F32),
            pltpu.VMEM((128, TOK), F32),
            pltpu.VMEM((TOK, 128), F32),
            pltpu.VMEM((TOK, WIDE), BF16),
            pltpu.VMEM((TOK, WIDE), BF16),
            pltpu.VMEM((8, TOK), F32),
            pltpu.VMEM((8, TOK), F32),
            pltpu.VMEM((2, 2, WIDE // 2, NSTATE), F32),
            pltpu.VMEM((2, 2, WIDE // 2, NSTATE), F32),
            pltpu.VMEM((CHIPS, 16, 128), BF16),
            pltpu.VMEM((CHIPS, 16, 128), BF16),
            pltpu.VMEM((CHIPS, 16, 128), F32),
            pltpu.VMEM((CHIPS, 16, 128), F32),
            pltpu.VMEM((CHIPS, 16, 128), BF16),
            pltpu.VMEM((2, CHIPS, 16, 128), BF16),
            pltpu.VMEM((2, CHIPS, 128), F32),
            pltpu.VMEM((2, 1, 128), F32),
            pltpu.VMEM((CHIPS, 1, 128), F32),
            pltpu.VMEM((2 * NHEAD, 1, 128), F32),
            pltpu.SemaphoreType.DMA((10,)),
            pltpu.SemaphoreType.DMA((2,)),
            pltpu.SemaphoreType.DMA((2,)),
            pltpu.SemaphoreType.DMA((count,)),
            pltpu.SemaphoreType.DMA((count,)),
            pltpu.SemaphoreType.DMA((2,)),
            pltpu.SemaphoreType.DMA((2,)),
        ],
        compiler_params=pltpu.CompilerParams(
            collective_id=0, has_side_effects=True, vmem_limit_bytes=VMEM_LIMIT
        ),
    )(hidden, w_bc, x_act, logp_dir, step_size, rate, skip, mask, base, stretches)


def finish_kernel(gx_ref, gstep_ref, gcols_ref, few_ref, sums_ref, stretch_ref, grad_x_ref, grad_step_ref, cols_ref, small_ref):
    index = lax.axis_index("ctx")
    one, two, three = sequence_starts(stretch_ref)
    sums = sums_ref[0:1]
    lane = lax.broadcasted_iota(jnp.int32, (1, 128), 1)
    base = jnp.where(index >= two, 2, 0)
    signed = jnp.where(lane == base, sums, 0.0) - jnp.where(lane == base + 1, sums, 0.0)
    margin = jnp.sum(signed, axis=1, keepdims=True)
    coef = 1.0 / (1.0 + jnp.exp(-hinge_sharp * (hinge_margin - margin)))
    rejected = ((index >= one) & (index < two)) | (index >= three)
    scale = jnp.where(rejected, coef, -coef)
    grad_x_ref[...] = (gx_ref[...] * scale).astype(BF16)
    grad_step_ref[...] = gstep_ref[...] * scale
    cols_ref[...] = (gcols_ref[...] * scale).astype(BF16)
    small_ref[...] = few_ref[...] * scale


def finish(gx, gstep, gcols, few, sums, stretches):
    vmem = pl.BlockSpec(memory_space=pltpu.VMEM)
    shape = jax.ShapeDtypeStruct
    return pl.pallas_call(
        finish_kernel,
        name="finish",
        out_shape=(
            shape((TOK, WIDE), BF16),
            shape((8, TOK), F32),
            shape((TOK, COLS), BF16),
            shape((8, 128), F32),
        ),
        in_specs=[vmem] * 5 + [pl.BlockSpec(memory_space=pltpu.SMEM)],
        out_specs=tuple([vmem] * 4),
        compiler_params=pltpu.CompilerParams(vmem_limit_bytes=16 << 20),
    )(gx, gstep, gcols, few, sums, stretches)


def reduce_kernel(
    hid_ref, cols_ref, few_ref, out_ref, total_ref,
    hid, prod, mate_out, mate_in, a_out, a_own, a_in, a2_out, a2_own, a2_in,
    b_out, b_own, b_in, b2_out, b2_own, b2_in, few, few_c, few_z, few_x, load_sem, ss, rs,
):
    x, z, c, head = place()
    load = pltpu.make_async_copy(hid_ref, hid, load_sem)
    load.start()
    greet(plane_partners(x, z, c, head))
    mate = at(x, z, 1 - c, head)
    started = []

    def send(source, target, k, partner):
        copy = pltpu.make_async_remote_copy(
            source, target, ss.at[k], rs.at[k], device_id=partner, device_id_type=MESH
        )
        copy.start()
        started.append(copy)
        return copy

    few[0] = few_ref[...]
    few_copy = send(few.at[0], few_c, 0, mate)
    load.wait()
    grads = cols_ref[...]
    span = MODEL // NX
    order = (2, 1, 3, 0)
    mate_copies = {}
    for dx in order:
        to = (x + dx) % NX
        chunk = hid[:, pl.ds(pl.multiple_of(to * span, span), span)]
        prod[dx] = dot(chunk, grads, ((0,), (0,))).reshape(NZ, NC, DEPTH, COLS)
        mate_out[dx] = prod[dx, :, 1 - c].astype(BF16)
        mate_copies[dx] = send(mate_out.at[dx], mate_in.at[dx], 1 + dx, mate)
    few_copy.wait_recv()
    few[1] = few[0] + few_c[...]
    few_copies = [
        send(few.at[1], few_z.at[dz - 1], 4 + dz, at(x, z + dz, c, head)) for dz in range(1, NZ)
    ]
    a_copies = []
    for dx in order:
        mate_copies[dx].wait_recv()
        chip = prod[dx, :, c] + mate_in[dx].astype(F32)
        b_own[dx] = chip[:, PART:]
        b_out[:, dx] = chip[:, PART:].astype(BF16)
        if dx:
            a_out[dx - 1] = chip[:, :PART].astype(BF16)
            a_copies.append(send(a_out.at[dx - 1], a_in.at[dx - 1], 11 + dx, at(x + dx, z, c, head)))
        else:
            a_own[...] = chip[:, :PART]
    b_copies = [
        send(b_out.at[(z + dz) % NZ], b_in.at[dz - 1], 14 + dz, at(x, z + dz, c, head))
        for dz in (4, 3, 5, 2, 6, 1, 7)
    ]
    for copy in few_copies:
        copy.wait_recv()
    few[2] = few[1] + jnp.sum(few_z[...], axis=0)
    few_copies = [
        send(few.at[2], few_x.at[dx - 1], 21 + dx, at(x + dx, z, c, head)) for dx in range(1, NX)
    ]
    for copy in b_copies:
        copy.wait_recv()
    b2_own[...] = b_own[:, z] + jnp.sum(b_in[...].astype(F32), axis=0)
    b2_out[...] = b2_own[...].astype(BF16)
    b2_copies = [
        send(b2_out.at[dx], b2_in.at[dx - 1], 24 + dx, at(x + dx, z, c, head)) for dx in range(1, NX)
    ]
    for copy in a_copies:
        copy.wait_recv()
    a2_own[...] = a_own[...] + jnp.sum(a_in[...].astype(F32), axis=0)
    a2_out[...] = a2_own[...].astype(BF16)
    a2_copies = [
        send(a2_out.at[(z + dz) % NZ], a2_in.at[dz - 1], 27 + dz, at(x, z + dz, c, head))
        for dz in (4, 3, 5, 2, 6, 1, 7)
    ]
    for copy in few_copies + b2_copies:
        copy.wait_recv()
    total_ref[...] = few[2] + jnp.sum(few_x[...], axis=0)
    out_ref[PART:] = b2_own[0] + jnp.sum(b2_in[...].astype(F32), axis=0)
    for copy in a2_copies:
        copy.wait_recv()
    out_ref[:PART] = a2_own[z] + jnp.sum(a2_in[...].astype(F32), axis=0)
    for copy in started:
        copy.wait_send()


def reduce_part(hidden, grad_cols, few):
    vmem = pl.BlockSpec(memory_space=pltpu.VMEM)
    shape = jax.ShapeDtypeStruct
    rest = DEPTH - PART
    return pl.pallas_call(
        reduce_kernel,
        name="reduce_part",
        out_shape=(shape((DEPTH, COLS), F32), shape((8, 128), F32)),
        in_specs=[pl.BlockSpec(memory_space=pl.ANY), vmem, vmem],
        out_specs=(vmem, vmem),
        scratch_shapes=[
            pltpu.VMEM((TOK, MODEL), BF16),
            pltpu.VMEM((NX, NZ, NC, DEPTH, COLS), F32),
            pltpu.VMEM((NX, NZ, DEPTH, COLS), BF16),
            pltpu.VMEM((NX, NZ, DEPTH, COLS), BF16),
            pltpu.VMEM((NX - 1, NZ, PART, COLS), BF16),
            pltpu.VMEM((NZ, PART, COLS), F32),
            pltpu.VMEM((NX - 1, NZ, PART, COLS), BF16),
            pltpu.VMEM((NZ, PART, COLS), BF16),
            pltpu.VMEM((NZ, PART, COLS), F32),
            pltpu.VMEM((NZ - 1, PART, COLS), BF16),
            pltpu.VMEM((NZ, NX, rest, COLS), BF16),
            pltpu.VMEM((NX, NZ, rest, COLS), F32),
            pltpu.VMEM((NZ - 1, NX, rest, COLS), BF16),
            pltpu.VMEM((NX, rest, COLS), BF16),
            pltpu.VMEM((NX, rest, COLS), F32),
            pltpu.VMEM((NX - 1, rest, COLS), BF16),
            pltpu.VMEM((3, 8, 128), F32),
            pltpu.VMEM((8, 128), F32),
            pltpu.VMEM((NZ - 1, 8, 128), F32),
            pltpu.VMEM((NX - 1, 8, 128), F32),
            pltpu.SemaphoreType.DMA,
            pltpu.SemaphoreType.DMA((35,)),
            pltpu.SemaphoreType.DMA((35,)),
        ],
        compiler_params=pltpu.CompilerParams(
            collective_id=2, has_side_effects=True, vmem_limit_bytes=VMEM_LIMIT
        ),
    )(hidden, grad_cols, few)


def body(
    hidden, w_bc, x_act, step_size, decay_rate, skip_gain, logp_dir, base_logp, seq_stretches, resp_mask
):
    gx, gstep, gcols, few, sums = front(
        hidden, w_bc, x_act, logp_dir, step_size, decay_rate, skip_gain,
        resp_mask.reshape(1, TOK), base_logp.reshape(1, TOK), seq_stretches,
    )
    grad_x, grad_step, grad_cols, few = finish(gx, gstep, gcols, few, sums, seq_stretches)
    grad_w, total = reduce_part(hidden, grad_cols, few)
    return grad_x, grad_step, total[0, :HEADS], total[1, :HEADS], grad_w


def solution(mesh):
    return jax.shard_map(
        body,
        mesh=mesh,
        in_specs=(
            P("ctx", None),
            P("ctx", "head"),
            P("ctx", "head"),
            P("head", "ctx"),
            P("head"),
            P("head"),
            P("ctx", "head"),
            P("ctx"),
            P(),
            P("ctx"),
        ),
        out_specs=(P("ctx", "head"), P("head", "ctx"), P("head"), P("head"), P("ctx", "head")),
        check_vma=False,
    )
```

```python
import functools

import jax
import jax.numpy as jnp
from jax import lax
from jax.experimental import pallas as pl
from jax.experimental.pallas import tpu as pltpu
from jax.sharding import PartitionSpec as P

HEADDIM = 64
NSTATE = 128
NX, NZ, NC = 4, 8, 2
NCTX = NX * NZ * NC
CHIPS = NX * NZ
NHEAD = 8
TOK = 256
HEADS = 8
WIDE = HEADS * HEADDIM
DEPTH = 64
COLS = 2 * NSTATE
MODEL = NCTX * DEPTH
PART = 48
AHEAD = 3

hinge_sharp = 0.005
hinge_margin = 10.0

FAR_FIRST = sorted(
    [(dx, dz) for dx in range(NX) for dz in range(NZ) if dx or dz],
    key=lambda step: -(min(step[0], NX - step[0]) + min(step[1], NZ - step[1])),
)

MESH = pl.DeviceIdType.MESH
F32 = jnp.float32
BF16 = jnp.bfloat16
VMEM_LIMIT = 64 << 20
SPACE = pltpu.HBM


def place():
    index = lax.axis_index("ctx")
    return index // 16, (index // 2) % 8, index % 2, lax.axis_index("head")


def at(x, z, c, head):
    return (((x % NX) * NZ + (z % NZ)) * NC + c, head)


def dot(left, right, dims=((1,), (0,)), precision=None):
    return lax.dot_general(left, right, (dims, ((), ())), precision=precision, preferred_element_type=F32)


def pair_columns(columns, base, pair, low_half):
    one, two = base + 2 * pair, base + 2 * pair + 1
    return jnp.where(low_half, columns[:, one : one + 1], columns[:, two : two + 1])


def sequence_starts(stretch_ref):
    one = stretch_ref[0]
    two = one + stretch_ref[1]
    return one, two, two + stretch_ref[2]


def halves(value):
    top = value.astype(BF16)
    return top, (value - top.astype(F32)).astype(BF16)


def keep_of(block, starts):
    begins = block == 0
    for start in starts:
        begins = begins | (block == start)
    return jnp.where(begins, 0.0, 1.0)


def seq_of(block, starts):
    return sum((block >= start).astype(jnp.int32) for start in starts)


def whole_kernel(
    hid_hbm, w_hbm, x_hbm, dir_hbm, step_hbm, rate_hbm, skip_hbm, mask_hbm, base_hbm, stretch_hbm,
    grad_x_out, grad_step_out, rate_out, skip_out, grad_w_out,
    hid, x_ref, dir_ref, step_ref, rate_ref, skip_ref, mask_ref, base_ref, stretch_ref,
    buf, dec, factors, moves, stack, cols_ref, xf_ref, dyg_ref, drow, dcol, lg, mate_lg, msg, got, wide,
    swept, reply, states, tab, part, near, across,
    gx_ref, gcols_ref, gx_bf, gstep_ref, gw_ref, small,
    prod, mate_out, mate_in, a_out, a_own, a_in, a2_out, a2_in, b_out, bz_in, b2_out, b2_in,
    few, few_c, few_z, few_x,
    load_sem, send_sem, recv_sem, ss, rs, gs, gr,
):
    index = lax.axis_index("ctx")
    x, z, c, head = place()
    chip = index // 2
    mate = at(x, z, 1 - c, head)
    every = slice(None)

    barrier = pltpu.get_barrier_semaphore()

    def hello(partner):
        pl.semaphore_signal(barrier, inc=1, device_id=partner, device_id_type=MESH)

    for dz in (4, 3, 5, 2, 6, 1, 7):
        hello(at(x, z + dz, c, head))
    for dx in (2, 1, 3):
        hello(at(x + dx, z, c, head))
    hello(mate)
    loads = {}
    for k, (name, source, target) in enumerate(
        (
            ("step", step_hbm, step_ref),
            ("rate", rate_hbm, rate_ref),
            ("w", w_hbm, buf.at[x, z, c]),
            ("mask", mask_hbm, mask_ref),
            ("x", x_hbm, x_ref),
            ("dir", dir_hbm, dir_ref),
            ("skip", skip_hbm, skip_ref),
            ("base", base_hbm, base_ref),
            ("stretch", stretch_hbm, stretch_ref),
            ("hid", hid_hbm, hid),
        )
    ):
        loads[name] = pltpu.make_async_copy(source, target, load_sem.at[k])
        loads[name].start()

    for k in range(2, 2 * NHEAD):
        hello((chip * 2 + (c + k) % 2, (head + k // 2) % NHEAD))
    loads["w"].wait()
    pl.semaphore_wait(barrier, NZ - 1 + NX - 1 + 2 * NHEAD - 1)

    started, slots = [], {}

    def slot(key):
        return slots.setdefault(key, len(slots))

    def send(ref, where, key, partner, into=None):
        k = slot(key)
        copy = pltpu.make_async_remote_copy(
            ref.at[where],
            (ref if into is None else into).at[where],
            ss.at[k],
            rs.at[k],
            device_id=partner,
            device_id_type=MESH,
        )
        copy.start()
        started.append(copy)

    def send_few(source, target, into, key, partner):
        k = slot(key)
        copy = pltpu.make_async_remote_copy(
            few.at[source], target.at[into], ss.at[k], rs.at[k], device_id=partner, device_id_type=MESH
        )
        copy.start()
        started.append(copy)

    def arrive(ref, where, key):
        piece = ref.at[where]
        k = slot(key)
        pltpu.make_async_remote_copy(
            piece, piece, ss.at[k], rs.at[k], device_id=mate, device_id_type=MESH
        ).wait_recv()

    low, high = pl.ds(0, PART), pl.ds(PART, DEPTH - PART)
    near_z, near_x = (1, 7, 2, 6, 3, 5, 4), (1, 3, 2)

    def to_z(dz):
        return at(x, z + dz, c, head)

    def to_x(dx):
        return at(x + dx, z, c, head)

    def from_z(dz):
        return (z - dz) % NZ

    def from_x(dx):
        return (x - dx) % NX

    for dz in near_z:
        send(buf, (x, z, c, low), ("az", dz), to_z(dz))
    for dx in near_x:
        send(buf, (x, z, c, high), ("bx", dx), to_x(dx))
    for dx in near_x:
        send(buf, (x, z, c, low), ("ax", 0, dx), to_x(dx))
    for dz in near_z:
        send(buf, (x, z, c, high), ("bz", 0, dz), to_z(dz))
    send(buf, (x, z, c), ("own",), mate)

    loads["step"].wait()
    loads["rate"].wait()
    rows8 = lax.broadcasted_iota(jnp.int32, (8, 128), 0)
    lanes8 = lax.broadcasted_iota(jnp.int32, (8, 128), 1)
    step = step_ref[...]
    row8 = lax.broadcasted_iota(jnp.int32, (8, TOK), 0)
    rate = jnp.zeros((8, TOK), F32)
    for h in range(HEADS):
        rate = jnp.where(row8 == h, rate_ref[h], rate)
    total = -rate[:, 0:1] * jnp.sum(step, axis=1, keepdims=True)
    dec[x, z, c] = jnp.sum(jnp.where(rows8 == lanes8, total, 0.0), axis=0, keepdims=True)
    for dz in near_z:
        send(dec, (x, z, c), ("dz", dz), to_z(dz))

    s_index = lax.broadcasted_iota(jnp.int32, (TOK, TOK), 0)
    t_index = lax.broadcasted_iota(jnp.int32, (TOK, TOK), 1)
    causal = s_index <= t_index
    cum = -rate * dot(step, causal.astype(F32), precision=lax.Precision.HIGHEST)
    last = cum[:, TOK - 1 : TOK]
    loads["mask"].wait()
    mask = mask_ref[...].astype(F32)
    stack[...] = jnp.zeros((128, TOK), F32)
    stack[0:8] = cum - jnp.log(step)
    stack[8:16] = jnp.exp(cum)
    stack[16:24] = jnp.exp(last - cum) * step
    stack[24:32] = jnp.broadcast_to(mask, (8, TOK))
    columns = stack[...].T
    cols_ref[...] = columns
    loads["x"].wait()
    loads["dir"].wait()
    loads["skip"].wait()
    loads["base"].wait()
    loads["stretch"].wait()
    low_half = lax.broadcasted_iota(jnp.int32, (TOK, 128), 1) < HEADDIM
    overlap = []

    def prepare(pair):
        columns = cols_ref[...]
        span = slice(128 * pair, 128 * pair + 128)
        x_pair = x_ref[:, span]
        x_wide = x_pair.astype(F32)
        dy_wide = dir_ref[:, span].astype(F32) * columns[:, 24:25]
        dy_pair = dy_wide.astype(BF16)
        dir_ref[:, span] = dy_pair
        xf_ref[:, span] = (x_wide * pair_columns(columns, 16, pair, low_half)).astype(BF16)
        dyg_ref[:, span] = (dy_wide * pair_columns(columns, 8, pair, low_half)).astype(BF16)
        overlap.append(jnp.sum(x_wide * dy_wide, axis=0, keepdims=True))
        for h in (2 * pair, 2 * pair + 1):
            half = slice(HEADDIM * (h % 2), HEADDIM * (h % 2) + HEADDIM)
            gap = jnp.where(causal, cum[h : h + 1, :] - columns[:, h : h + 1], -1e30)
            factor = jnp.exp(gap)
            factors[h] = factor
            moves[h] = dot(x_pair[:, half], dy_pair[:, half], ((1,), (1,))) * factor
        skip_pair = jnp.where(low_half, skip_ref[2 * pair], skip_ref[2 * pair + 1])
        gx_ref[:, span] = skip_pair * dy_wide

    def forward_low(dz):
        where = (x, from_z(dz), c, low)
        arrive(buf, where, ("az", dz))
        for dx in near_x:
            send(buf, where, ("ax", dz, dx), to_x(dx))
        send(buf, where, ("am", dz), mate)

    def forward_high(dx):
        where = (from_x(dx), z, c, high)
        arrive(buf, where, ("bx", dx))
        for dz in near_z:
            send(buf, where, ("bz", dx, dz), to_z(dz))
        send(buf, where, ("bm", dx), mate)

    def take_low(dz, dx):
        where = (from_x(dx), from_z(dz), c, low)
        arrive(buf, where, ("ax", dz, dx))
        send(buf, where, ("axm", dz, dx), mate)

    def take_high(dz):
        for dx in (0, 1, 3, 2):
            arrive(buf, (from_x(dx), from_z(dz), c, high), ("bz", dx, dz))
        send(buf, (every, from_z(dz), c, high), ("bzm", dz), mate)

    prepare(0)
    for dz in (1, 7):
        forward_low(dz)
    for dx in (1, 3):
        forward_high(dx)
    prepare(1)
    for dz in (2, 6):
        forward_low(dz)
    forward_high(2)
    prepare(2)
    for dz in (3, 5, 4):
        forward_low(dz)
    for dz in near_z:
        arrive(dec, (x, from_z(dz), c), ("dz", dz))
    for dx in near_x:
        send(dec, (x, every, c), ("dx", dx), to_x(dx))
    prepare(3)
    for dx in near_x:
        take_low(0, dx)
    for dz in (1, 7):
        for dx in near_x:
            take_low(dz, dx)
    for dz in (1, 7):
        take_high(dz)
    for dz in (2, 6):
        for dx in near_x:
            take_low(dz, dx)
    for dz in (2, 6):
        take_high(dz)
    for dx in near_x:
        arrive(dec, (from_x(dx), every, c), ("dx", dx))
    send(dec, (every, every, c), ("dm",), mate)
    for dz in (3, 5, 4):
        for dx in near_x:
            take_low(dz, dx)
        take_high(dz)

    other = 1 - c
    arrive(buf, (x, z, other), ("own",))
    for dz in near_z:
        arrive(buf, (x, from_z(dz), other, low), ("am", dz))
    for dx in near_x:
        arrive(buf, (from_x(dx), z, other, high), ("bm", dx))
    for dz in (0,) + near_z:
        for dx in near_x:
            arrive(buf, (from_x(dx), from_z(dz), other, low), ("axm", dz, dx))
    for dz in near_z:
        arrive(buf, (every, from_z(dz), other, high), ("bzm", dz))
    loads["hid"].wait()
    span = MODEL // NX
    sums = jnp.zeros((TOK, COLS), F32)
    for k in range(NX):
        sums = sums + dot(hid[:, k * span : (k + 1) * span], buf[k].reshape(span, COLS))
    bc = sums.astype(BF16)
    b_in, c_in = bc[:, :NSTATE], bc[:, NSTATE:]
    lg[0] = dot(xf_ref[...], b_in, ((0,), (0,))).reshape(2, WIDE // 2, NSTATE)
    lg[1] = dot(dyg_ref[...], c_in, ((0,), (0,))).reshape(2, WIDE // 2, NSTATE)
    send(lg, (every, other), ("l1",), mate, mate_lg)
    send(lg, (every, c), ("l2",), mate, mate_lg)

    starts = sequence_starts(stretch_ref)
    arrive(dec, (every, every, other), ("dm",))
    row0, row1 = jnp.exp(dec[x, z, 0]), jnp.exp(dec[x, z, 1])
    lane1 = lax.broadcasted_iota(jnp.int32, (1, 128), 1)

    def pick(row, h):
        return jnp.sum(jnp.where(lane1 == h, row, 0.0), axis=1, keepdims=True)

    keep0, keep1 = keep_of(2 * chip, starts), keep_of(2 * chip + 1, starts)
    next1 = jnp.where(2 * chip + 2 == NCTX, 0.0, keep_of(2 * chip + 2, starts))
    first = c == 0
    arrive(mate_lg, (every, c), ("l1",))
    met = jnp.zeros((HEADDIM, 128), F32)
    chip_l, chip_g = [], []
    for hh in range(HEADS // 2):
        span = slice(HEADDIM * hh, HEADDIM * hh + HEADDIM)
        mine_l, mine_g = lg[0, c, span], lg[1, c, span]
        mate_l, mate_g = mate_lg[0, c, span], mate_lg[1, c, span]
        l0, l1 = jnp.where(first, mine_l, mate_l), jnp.where(first, mate_l, mine_l)
        g0, g1 = jnp.where(first, mine_g, mate_g), jnp.where(first, mate_g, mine_g)
        h = 4 * c + hh
        chip_l.append(pick(row1, h) * keep1 * l0 + l1)
        chip_g.append(pick(row0, h) * keep1 * g1 + g0)
        met = met + l0 * g1
    msg[...] = jnp.concatenate(
        [
            jnp.concatenate(chip_l, axis=0).reshape(CHIPS, 8, 128),
            jnp.concatenate(chip_g, axis=0).reshape(CHIPS, 8, 128),
        ],
        axis=1,
    ).astype(BF16)

    def exchange(source, target, phase):
        for dx, dz in FAR_FIRST:
            to = ((x + dx) % NX) * NZ + (z + dz) % NZ
            pltpu.make_async_remote_copy(
                source.at[to],
                target.at[chip],
                send_sem.at[phase],
                recv_sem.at[phase],
                device_id=(to * 2 + c, head),
                device_id_type=MESH,
            ).start()

    def settle(target, sem):
        rest = target.at[pl.ds(0, CHIPS - 1)]
        pltpu.make_async_copy(rest, rest, sem).wait()

    exchange(msg, got, 0)
    got[chip] = msg[chip]

    scores = dot(b_in, c_in, ((1,), (1,)))
    grad_scores = jnp.zeros((TOK, TOK), F32)
    back = jnp.zeros((TOK, 128), F32)
    lane128 = lax.broadcasted_iota(jnp.int32, (TOK, 128), 1)
    for pair in range(HEADS // 2):
        span = slice(128 * pair, 128 * pair + 128)
        within = []
        for h in (2 * pair, 2 * pair + 1):
            moved = moves[h]
            grad_scores = grad_scores + moved
            spent = moved * scores
            drow[h : h + 1] = jnp.sum(spent, axis=0, keepdims=True)
            back = jnp.where(lane128 == h, jnp.sum(spent, axis=1, keepdims=True), back)
            dy_h = dir_ref[:, HEADDIM * h : HEADDIM * h + HEADDIM]
            within.append(dot((scores * factors[h]).astype(BF16), dy_h))
        gx_ref[:, span] = gx_ref[:, span] + jnp.concatenate(within, axis=1)
    dcol[...] = back.T[0:8]
    grad_bf = grad_scores.astype(BF16)
    gcols_ref[:, :NSTATE] = dot(grad_bf, c_in)
    gcols_ref[:, NSTATE:] = dot(grad_bf, b_in, ((0,), (0,)))

    wide_row = lax.broadcasted_iota(jnp.int32, (WIDE, 128), 0) // HEADDIM
    wide_lane = lax.broadcasted_iota(jnp.int32, (WIDE, 128), 1)
    overlap_row = jnp.broadcast_to(jnp.concatenate(overlap, axis=1), (8, WIDE))
    overlap_head = dot(overlap_row, (wide_row == wide_lane).astype(F32), precision=lax.Precision.HIGHEST)
    skip_row = jnp.zeros((1, 128), F32)
    for h in range(HEADS):
        skip_row = jnp.where(lane1 == h, skip_ref[h], skip_row)
    pieces = jnp.sum(grad_scores * scores, axis=0, keepdims=True)
    pieces = pieces + jnp.where(head == 0, 1.0, 0.0) * mask * base_ref[...]
    own = pieces[:, :128] + pieces[:, 128:] + overlap_head[0:1] * skip_row
    own = jnp.sum(own, axis=1, keepdims=True)
    pair_sum = keep1 * jnp.sum(jnp.sum(met, axis=0, keepdims=True), axis=1, keepdims=True)
    mine = jnp.where(lane1 == seq_of(index, starts), own, 0.0)
    mine = mine + jnp.where(lane1 == seq_of(2 * chip + 1, starts), pair_sum, 0.0)

    chips = lax.broadcasted_iota(jnp.int32, (CHIPS, 128), 0)
    lane32 = lax.broadcasted_iota(jnp.int32, (CHIPS, 128), 1)
    my_head = 4 * c + chip // 8

    def decays(core):
        table = jnp.concatenate([dec[m // NZ, m % NZ, core] for m in range(CHIPS)], axis=0)
        return jnp.exp(jnp.sum(jnp.where(lane32 == my_head, table, 0.0), axis=1, keepdims=True))

    both = decays(0) * decays(1) * keep_of(2 * chips + 1, starts)
    enters = keep_of(2 * chips, starts)
    tab[0] = both * enters
    tab[1] = both * jnp.where(chips == CHIPS - 1, 0.0, keep_of(2 * chips + 2, starts))

    settle(got, recv_sem.at[0])
    wide[...] = got[...].astype(F32)

    def advance(b, carry):
        state, grad = carry
        r = CHIPS - 1 - b
        swept[b, 0:8] = state
        swept[r, 8:16] = grad
        state = state * tab[0, pl.ds(b, 1)] + wide[b, 0:8]
        grad = grad * tab[1, pl.ds(r, 1)] + wide[r, 8:16]
        return state, grad

    zero = jnp.zeros((8, 128), F32)
    lax.fori_loop(0, CHIPS, advance, (zero, zero))
    met = jnp.sum(swept[:, 0:8] * wide[:, 8:16], axis=1) * enters
    met = jnp.sum(met, axis=1, keepdims=True)
    seqs = seq_of(2 * chips, starts)
    mine = mine + jnp.sum(jnp.where(lane32 == seqs, met, 0.0), axis=0, keepdims=True)
    part[0] = mine

    for k, (dx, dz) in enumerate(FAR_FIRST):
        to = ((x + dx) % NX) * NZ + (z + dz) % NZ
        pltpu.make_async_remote_copy(
            part.at[0],
            near.at[k + 1],
            gs.at[0],
            gr.at[0],
            device_id=(to * 2 + c, head),
            device_id_type=MESH,
        ).start()
    near[0] = mine
    reply[...] = swept[...].astype(BF16)
    exchange(reply, states.at[c], 1)
    states[c, chip] = reply[chip]

    def settle_few(target, sem, count):
        rest = target.at[pl.ds(1, count)]
        pltpu.make_async_copy(rest, rest, sem).wait()

    settle_few(near, gr.at[0], CHIPS - 1)
    gathered = jnp.sum(near[...], axis=0)
    part[1] = gathered

    def spread_head(k, carry):
        to = (head + k // 2) % NHEAD
        who = chip * 2 + (c + k) % 2
        pltpu.make_async_remote_copy(
            part.at[1], across.at[k], gs.at[1], gr.at[1], device_id=(who, to), device_id_type=MESH
        ).start()
        return carry

    lax.fori_loop(1, 2 * NHEAD, spread_head, 0)
    across[0] = gathered

    settle(states.at[c], recv_sem.at[1])
    send(states, (c,), ("st",), mate)
    arrive(mate_lg, (every, other), ("l2",))

    def spaced(row):
        return jnp.concatenate(
            [jnp.broadcast_to(pick(row, h), (HEADDIM, 128)) for h in range(HEADS)], axis=0
        )

    lead = jnp.where(first, keep0, keep0 * keep1 * spaced(row0))
    lead_mate = jnp.where(first, 0.0, keep1)
    trail = jnp.where(first, next1 * keep1 * spaced(row1), next1)
    trail_mate = jnp.where(first, keep1, 0.0)
    arrive(states, (other,), ("st",))
    states_f = states[...].astype(F32)
    state_in = lead * states_f[:, :, 0:8].reshape(WIDE, NSTATE)
    state_in = state_in + lead_mate * mate_lg[0].reshape(WIDE, NSTATE)
    grad_state = trail * states_f[:, :, 8:16].reshape(WIDE, NSTATE)
    grad_state = grad_state + trail_mate * mate_lg[1].reshape(WIDE, NSTATE)

    columns = cols_ref[...]
    state_bf, gstate_bf = state_in.astype(BF16), grad_state.astype(BF16)
    pick_half = lanes8 // HEADDIM
    nt = ((1,), (1,))
    carried = jnp.zeros((8, TOK), F32)
    kept = jnp.zeros((8, TOK), F32)
    for pair in range(HEADS // 2):
        span = slice(128 * pair, 128 * pair + 128)
        picks = (rows8 == 2 * pair + pick_half).astype(BF16)
        top, rest = halves(dot(c_in, state_bf[span], nt) * dyg_ref[:, span].astype(F32))
        carried = carried + dot(picks, top, nt) + dot(picks, rest, nt)
        pulled = dot(b_in, gstate_bf[span], nt) * pair_columns(columns, 16, pair, low_half)
        top, rest = halves(pulled * x_ref[:, span].astype(F32))
        kept = kept + dot(picks, top, nt) + dot(picks, rest, nt)
        gx_ref[:, span] = gx_ref[:, span] + pulled
    gcols_ref[:, :NSTATE] = gcols_ref[:, :NSTATE] + dot(xf_ref[...], gstate_bf)
    gcols_ref[:, NSTATE:] = gcols_ref[:, NSTATE:] + dot(dyg_ref[...], state_bf)

    grad_decay = jnp.sum(
        jnp.sum((state_in * grad_state).reshape(HEADS, HEADDIM, NSTATE), axis=1), axis=1, keepdims=True
    )
    end = jnp.sum(kept, axis=1, keepdims=True) + grad_decay * jnp.exp(last)
    token = lax.broadcasted_iota(jnp.int32, (8, TOK), 1)
    grad_cum = drow[...] - dcol[...] + carried - kept + jnp.where(token == TOK - 1, end, 0.0)
    tail = dot(grad_cum, (s_index >= t_index).astype(F32), precision=lax.Precision.HIGHEST)
    grad_step = (dcol[...] + kept) / step - rate * tail
    grad_rate = -jnp.sum(step * tail, axis=1, keepdims=True)
    rate_row = jnp.sum(jnp.where(lanes8 == rows8, grad_rate, 0.0), axis=0, keepdims=True)

    grads = gcols_ref[...].astype(BF16)
    order = (4, 3, 5, 2, 6, 1, 7, 0)

    def multiply(k):
        zz = (z + order[k]) % NZ
        for dx in range(NX):
            first_column = (((x + dx) % NX) * NZ + zz) * (NC * DEPTH)
            chunk = hid[:, pl.ds(pl.multiple_of(first_column, NC * DEPTH), NC * DEPTH)]
            prod[k, dx] = dot(chunk, grads, ((0,), (0,))).reshape(NC, DEPTH, COLS)
            mate_out[k, dx] = prod[k, dx, other].astype(BF16)
        send(mate_out, (k,), ("m", k), mate, mate_in)

    def scale_of(block, seq_sums):
        one, two, three = starts
        chosen = jnp.where(block >= two, 2, 0)
        signed = jnp.where(lane1 == chosen, seq_sums, 0.0) - jnp.where(lane1 == chosen + 1, seq_sums, 0.0)
        margin = jnp.sum(signed, axis=1, keepdims=True)
        coef = 1.0 / (1.0 + jnp.exp(-hinge_sharp * (hinge_margin - margin)))
        rejected = ((block >= one) & (block < two)) | (block >= three)
        return jnp.where(rejected, coef, -coef)

    def combine(k):
        dz = order[k]
        arrive(mate_in, (k,), ("m", k))
        for dx in (2, 1, 3):
            both = prod[k, dx, c] * scale + mate_in[k, dx].astype(F32) * scale_mate
            a_out[k, dx - 1] = both[:PART].astype(BF16)
            send(a_out, (k, dx - 1), ("a", k, dx), to_x(dx), a_in)
            prod[k, dx, c, PART:] = both[PART:]
        both = prod[k, 0, c] * scale + mate_in[k, 0].astype(F32) * scale_mate
        a_own[k] = both[:PART]
        prod[k, 0, c, PART:] = both[PART:]
        if dz:
            b_out[k] = prod[k, :, c, PART:].astype(BF16)
            send(b_out, (k,), ("b", k), to_z(dz), bz_in)

    def pass_on(k):
        dz = order[k]
        for dx in (1, 2, 3):
            arrive(a_in, (k, dx - 1), ("a", k, dx))
        a_own[k] = a_own[k] + jnp.sum(a_in[k].astype(F32), axis=0)
        if dz:
            a2_out[k] = a_own[k].astype(BF16)
            send(a2_out, (k,), ("a2", k), to_z(dz), a2_in)

    for k in range(AHEAD):
        multiply(k)
    settle_few(across, gr.at[1], 2 * NHEAD - 1)
    seq_sums = jnp.sum(across[...], axis=0)
    scale, scale_mate = scale_of(index, seq_sums), scale_of(index + 1 - 2 * c, seq_sums)
    for k in range(NZ):
        combine(k)
        if k + AHEAD < NZ:
            multiply(k + AHEAD)

    few[0] = jnp.where(rows8 == 0, rate_row, overlap_head) * scale
    send(few, (0,), ("fc",), mate, few_c)
    gx_bf[...] = (gx_ref[...] * scale).astype(BF16)
    gstep_ref[...] = grad_step * scale
    stores = [
        pltpu.make_async_copy(gx_bf, grad_x_out, load_sem.at[0]),
        pltpu.make_async_copy(gstep_ref, grad_step_out, load_sem.at[1]),
    ]
    for store in stores:
        store.start()
    arrive(few_c, (0,), ("fc",))
    few[1] = few[0] + few_c[0]

    pass_on(0)
    for dz in near_z:
        send_few(1, few_z, dz - 1, ("fz", dz), to_z(dz))
    for k in range(1, 4):
        pass_on(k)
    for dz in near_z:
        arrive(few_z, (dz - 1,), ("fz", dz))
    few[2] = few[1] + jnp.sum(few_z[...], axis=0)
    for dx in near_x:
        send_few(2, few_x, dx - 1, ("fx", dx), to_x(dx))
    pass_on(4)
    b_sum = prod[NZ - 1, :, c, PART:]
    for k in range(NZ - 1):
        arrive(bz_in, (k,), ("b", k))
        b_sum = b_sum + bz_in[k].astype(F32)
    for dx in (2, 1, 3):
        b2_out[dx - 1] = b_sum[dx].astype(BF16)
        send(b2_out, (dx - 1,), ("b2", dx), to_x(dx), b2_in)
    for k in range(5, NZ):
        pass_on(k)
    for dx in near_x:
        arrive(few_x, (dx - 1,), ("fx", dx))
    small[...] = few[2] + jnp.sum(few_x[...], axis=0)
    for h in range(HEADS):
        rate_ref[h] = small[0, h]
        skip_ref[h] = small[1, h]
    stores.append(pltpu.make_async_copy(rate_ref, rate_out, load_sem.at[2]))
    stores.append(pltpu.make_async_copy(skip_ref, skip_out, load_sem.at[4]))
    stores[-2].start()
    stores[-1].start()
    for dx in near_x:
        arrive(b2_in, (dx - 1,), ("b2", dx))
    gw_ref[PART:] = b_sum[0] + jnp.sum(b2_in[...].astype(F32), axis=0)
    a_sum = a_own[NZ - 1]
    for k in range(NZ - 1):
        arrive(a2_in, (k,), ("a2", k))
        a_sum = a_sum + a2_in[k].astype(F32)
    gw_ref[:PART] = a_sum
    stores.append(pltpu.make_async_copy(gw_ref, grad_w_out, load_sem.at[3]))
    stores[-1].start()

    for copy in started:
        copy.wait_send()
    settle(msg, send_sem.at[0])
    settle(reply, send_sem.at[1])
    settle_few(near, gs.at[0], CHIPS - 1)
    settle_few(across, gs.at[1], 2 * NHEAD - 1)
    for store in stores:
        store.wait()


def whole(hidden, w_bc, x_act, logp_dir, step_size, rate, skip, mask, base, stretches):
    shape = jax.ShapeDtypeStruct
    rest = DEPTH - PART
    count = 190
    return pl.pallas_call(
        whole_kernel,
        name="whole",
        out_shape=(
            shape((TOK, WIDE), BF16),
            shape((8, TOK), F32),
            shape((HEADS,), F32),
            shape((HEADS,), F32),
            shape((DEPTH, COLS), F32),
        ),
        in_specs=[pl.BlockSpec(memory_space=SPACE)] * 10,
        out_specs=tuple([pl.BlockSpec(memory_space=SPACE)] * 5),
        scratch_shapes=[
            pltpu.VMEM((TOK, MODEL), BF16),
            pltpu.VMEM((TOK, WIDE), BF16),
            pltpu.VMEM((TOK, WIDE), BF16),
            pltpu.VMEM((8, TOK), F32),
            pltpu.SMEM((8,), F32),
            pltpu.SMEM((8,), F32),
            pltpu.VMEM((1, TOK), jnp.int32),
            pltpu.VMEM((1, TOK), F32),
            pltpu.SMEM((4,), jnp.int32),
            pltpu.VMEM((NX, NZ, NC, DEPTH, COLS), BF16),
            pltpu.VMEM((NX, NZ, NC, 1, 128), F32),
            pltpu.VMEM((HEADS, TOK, TOK), F32),
            pltpu.VMEM((HEADS, TOK, TOK), F32),
            pltpu.VMEM((128, TOK), F32),
            pltpu.VMEM((TOK, 128), F32),
            pltpu.VMEM((TOK, WIDE), BF16),
            pltpu.VMEM((TOK, WIDE), BF16),
            pltpu.VMEM((8, TOK), F32),
            pltpu.VMEM((8, TOK), F32),
            pltpu.VMEM((2, 2, WIDE // 2, NSTATE), F32),
            pltpu.VMEM((2, 2, WIDE // 2, NSTATE), F32),
            pltpu.VMEM((CHIPS, 16, 128), BF16),
            pltpu.VMEM((CHIPS, 16, 128), BF16),
            pltpu.VMEM((CHIPS, 16, 128), F32),
            pltpu.VMEM((CHIPS, 16, 128), F32),
            pltpu.VMEM((CHIPS, 16, 128), BF16),
            pltpu.VMEM((2, CHIPS, 16, 128), BF16),
            pltpu.VMEM((2, CHIPS, 128), F32),
            pltpu.VMEM((2, 1, 128), F32),
            pltpu.VMEM((CHIPS, 1, 128), F32),
            pltpu.VMEM((2 * NHEAD, 1, 128), F32),
            pltpu.VMEM((TOK, WIDE), F32),
            pltpu.VMEM((TOK, COLS), F32),
            pltpu.VMEM((TOK, WIDE), BF16),
            pltpu.VMEM((8, TOK), F32),
            pltpu.VMEM((DEPTH, COLS), F32),
            pltpu.VMEM((8, 128), F32),
            pltpu.VMEM((NZ, NX, NC, DEPTH, COLS), F32),
            pltpu.VMEM((NZ, NX, DEPTH, COLS), BF16),
            pltpu.VMEM((NZ, NX, DEPTH, COLS), BF16),
            pltpu.VMEM((NZ, NX - 1, PART, COLS), BF16),
            pltpu.VMEM((NZ, PART, COLS), F32),
            pltpu.VMEM((NZ, NX - 1, PART, COLS), BF16),
            pltpu.VMEM((NZ - 1, PART, COLS), BF16),
            pltpu.VMEM((NZ - 1, PART, COLS), BF16),
            pltpu.VMEM((NZ - 1, NX, rest, COLS), BF16),
            pltpu.VMEM((NZ - 1, NX, rest, COLS), BF16),
            pltpu.VMEM((NX - 1, rest, COLS), BF16),
            pltpu.VMEM((NX - 1, rest, COLS), BF16),
            pltpu.VMEM((3, 8, 128), F32),
            pltpu.VMEM((1, 8, 128), F32),
            pltpu.VMEM((NZ - 1, 8, 128), F32),
            pltpu.VMEM((NX - 1, 8, 128), F32),
            pltpu.SemaphoreType.DMA((10,)),
            pltpu.SemaphoreType.DMA((2,)),
            pltpu.SemaphoreType.DMA((2,)),
            pltpu.SemaphoreType.DMA((count,)),
            pltpu.SemaphoreType.DMA((count,)),
            pltpu.SemaphoreType.DMA((2,)),
            pltpu.SemaphoreType.DMA((2,)),
        ],
        compiler_params=pltpu.CompilerParams(
            collective_id=0, has_side_effects=True, vmem_limit_bytes=VMEM_LIMIT
        ),
    )(hidden, w_bc, x_act, logp_dir, step_size, rate, skip, mask, base, stretches)


def finish_kernel(*refs):
    *ends, sems = refs
    count = len(ends) // 3
    sources, targets, holds = ends[:count], ends[count : 2 * count], ends[2 * count :]
    into = [pltpu.make_async_copy(sources[k], holds[k], sems.at[k]) for k in range(count)]
    back = [pltpu.make_async_copy(holds[k], targets[k], sems.at[count + k]) for k in range(count)]
    for copy in into:
        copy.start()
    for k in reversed(range(count)):
        into[k].wait()
        back[k].start()
    for copy in back:
        copy.wait()


def finish(*arrays):
    spec = pl.BlockSpec(memory_space=SPACE)
    return pl.pallas_call(
        finish_kernel,
        name="finish",
        out_shape=tuple(jax.ShapeDtypeStruct(array.shape, array.dtype) for array in arrays),
        in_specs=[spec] * len(arrays),
        out_specs=tuple([spec] * len(arrays)),
        scratch_shapes=[
            (pltpu.VMEM if array.ndim == 2 else pltpu.SMEM)(array.shape, array.dtype) for array in arrays
        ]
        + [pltpu.SemaphoreType.DMA((2 * len(arrays),))],
        compiler_params=pltpu.CompilerParams(vmem_limit_bytes=VMEM_LIMIT),
    )(*arrays)


def body(
    hidden, w_bc, x_act, step_size, decay_rate, skip_gain, logp_dir, base_logp, seq_stretches, resp_mask
):
    return finish(
        *whole(
            hidden, w_bc, x_act, logp_dir, step_size, decay_rate, skip_gain,
            resp_mask.reshape(1, TOK), base_logp.reshape(1, TOK), seq_stretches,
        )
    )


def solution(mesh):
    return jax.shard_map(
        body,
        mesh=mesh,
        in_specs=(
            P("ctx", None),
            P("ctx", "head"),
            P("ctx", "head"),
            P("head", "ctx"),
            P("head"),
            P("head"),
            P("ctx", "head"),
            P("ctx"),
            P(),
            P("ctx"),
        ),
        out_specs=(P("ctx", "head"), P("head", "ctx"), P("head"), P("head"), P("ctx", "head")),
        check_vma=False,
    )
```

```python
import functools

import jax
import jax.numpy as jnp
from jax import lax
from jax.experimental import pallas as pl
from jax.experimental.pallas import tpu as pltpu
from jax.sharding import PartitionSpec as P

HEADDIM = 64
NSTATE = 128
NX, NZ, NC = 4, 8, 2
NCTX = NX * NZ * NC
CHIPS = NX * NZ
NHEAD = 8
TOK = 256
HEADS = 8
WIDE = HEADS * HEADDIM
DEPTH = 64
COLS = 2 * NSTATE
MODEL = NCTX * DEPTH
PART = 48
AHEAD = 4

hinge_sharp = 0.005
hinge_margin = 10.0

FAR_FIRST = sorted(
    [(dx, dz) for dx in range(NX) for dz in range(NZ) if dx or dz],
    key=lambda step: -(min(step[0], NX - step[0]) + min(step[1], NZ - step[1])),
)

HEADS_FAR_FIRST = (8, 9, 6, 7, 10, 11, 4, 5, 12, 13, 2, 3, 14, 15, 1)

MESH = pl.DeviceIdType.MESH
F32 = jnp.float32
BF16 = jnp.bfloat16
VMEM_LIMIT = 64 << 20
SPACE = pltpu.HBM


def place():
    index = lax.axis_index("ctx")
    return index // 16, (index // 2) % 8, index % 2, lax.axis_index("head")


def at(x, z, c, head):
    return (((x % NX) * NZ + (z % NZ)) * NC + c, head)


def dot(left, right, dims=((1,), (0,)), precision=None):
    return lax.dot_general(left, right, (dims, ((), ())), precision=precision, preferred_element_type=F32)


def pair_columns(columns, base, pair, low_half):
    one, two = base + 2 * pair, base + 2 * pair + 1
    return jnp.where(low_half, columns[:, one : one + 1], columns[:, two : two + 1])


def sequence_starts(stretch_ref):
    one = stretch_ref[0]
    two = one + stretch_ref[1]
    return one, two, two + stretch_ref[2]


def halves(value):
    top = value.astype(BF16)
    return top, (value - top.astype(F32)).astype(BF16)


def keep_of(block, starts):
    begins = block == 0
    for start in starts:
        begins = begins | (block == start)
    return jnp.where(begins, 0.0, 1.0)


def seq_of(block, starts):
    return sum((block >= start).astype(jnp.int32) for start in starts)


def whole_kernel(
    hid_hbm, w_hbm, x_hbm, dir_hbm, step_hbm, rate_hbm, skip_hbm, mask_hbm, base_hbm, stretch_hbm,
    grad_x_out, grad_step_out, rate_out, skip_out, grad_w_out,
    hid, x_ref, dir_ref, step_ref, rate_ref, skip_ref, mask_ref, base_ref, stretch_ref,
    buf, dec, factors, moves, stack, cols_ref, xf_ref, dyg_ref, drow, dcol, lg, mate_lg, msg, got, wide,
    swept, reply, states, tab, part, near, across,
    hid_t, xf_t, dyg_t, gx_ref, gcols_ref, gx_bf, gstep_ref, gw_ref,
    prod, mate_out, mate_in, a_out, a_own, a_in, a2_out, a2_in, b_out, bz_in, b2_out, b2_in,
    few, few_c, few_all,
    load_sem, send_sem, recv_sem, ss, rs, gs, gr,
):
    index = lax.axis_index("ctx")
    x, z, c, head = place()
    chip = index // 2
    mate = at(x, z, 1 - c, head)
    every = slice(None)

    barrier = pltpu.get_barrier_semaphore()

    def hello(partner):
        pl.semaphore_signal(barrier, inc=1, device_id=partner, device_id_type=MESH)

    for dz in (4, 3, 5, 2, 6, 1, 7):
        hello(at(x, z + dz, c, head))
    for dx in (2, 1, 3):
        hello(at(x + dx, z, c, head))
    hello(mate)
    loads = {}
    for k, (name, source, target) in enumerate(
        (
            ("step", step_hbm, step_ref),
            ("rate", rate_hbm, rate_ref),
            ("w", w_hbm, buf.at[x, z, c]),
            ("mask", mask_hbm, mask_ref),
            ("x", x_hbm, x_ref),
            ("dir", dir_hbm, dir_ref),
            ("skip", skip_hbm, skip_ref),
            ("base", base_hbm, base_ref),
            ("stretch", stretch_hbm, stretch_ref),
            ("hid", hid_hbm, hid),
        )
    ):
        loads[name] = pltpu.make_async_copy(source, target, load_sem.at[k])
        loads[name].start()

    for k in range(2, 2 * NHEAD):
        hello((chip * 2 + (c + k) % 2, (head + k // 2) % NHEAD))
    loads["w"].wait()
    pl.semaphore_wait(barrier, NZ - 1 + NX - 1 + 2 * NHEAD - 1)

    sent, landed = {}, {}

    def slot(table, key):
        return table.setdefault(key, len(table))

    def move(source, target, out, key, partner):
        pltpu.make_async_remote_copy(
            source,
            target,
            ss.at[slot(sent, out)],
            rs.at[slot(landed, key)],
            device_id=partner,
            device_id_type=MESH,
        ).start()

    def send(ref, where, out, key, partner, into=None):
        move(ref.at[where], (ref if into is None else into).at[where], out, key, partner)

    def arrive(ref, where, key):
        piece = ref.at[where]
        pltpu.make_async_copy(piece, piece, rs.at[slot(landed, key)]).wait()

    def drain(out, piece):
        pltpu.make_async_copy(piece, piece, ss.at[sent.pop(out)]).wait()

    low, high = pl.ds(0, PART), pl.ds(PART, DEPTH - PART)
    near_z, near_x = (1, 7, 2, 6, 3, 5, 4), (1, 3, 2)
    far_z, far_x = (4, 3, 5, 2, 6, 1, 7), (2, 1, 3)

    def to_z(dz):
        return at(x, z + dz, c, head)

    def to_x(dx):
        return at(x + dx, z, c, head)

    def from_z(dz):
        return (z - dz) % NZ

    def from_x(dx):
        return (x - dx) % NX

    for dz in near_z:
        send(buf, (x, z, c, low), "plane", ("az", dz), to_z(dz))
    for dx in near_x:
        send(buf, (x, z, c, high), "plane", ("bx", dx), to_x(dx))
    for dx in near_x:
        send(buf, (x, z, c, low), "plane", ("ax", 0), to_x(dx))
    for dz in far_z:
        send(buf, (x, z, c, high), "plane", ("bz", dz), to_z(dz))
    send(buf, (x, z, c), "mate", "mate", mate)

    loads["step"].wait()
    loads["rate"].wait()
    rows8 = lax.broadcasted_iota(jnp.int32, (8, 128), 0)
    lanes8 = lax.broadcasted_iota(jnp.int32, (8, 128), 1)
    step = step_ref[...]
    row8 = lax.broadcasted_iota(jnp.int32, (8, TOK), 0)
    rate = jnp.zeros((8, TOK), F32)
    for h in range(HEADS):
        rate = jnp.where(row8 == h, rate_ref[h], rate)
    total = -rate[:, 0:1] * jnp.sum(step, axis=1, keepdims=True)
    dec[x, z, c] = jnp.sum(jnp.where(rows8 == lanes8, total, 0.0), axis=0, keepdims=True)
    for dz in near_z:
        send(dec, (x, z, c), "dz", "dz", to_z(dz))

    s_index = lax.broadcasted_iota(jnp.int32, (TOK, TOK), 0)
    t_index = lax.broadcasted_iota(jnp.int32, (TOK, TOK), 1)
    causal = s_index <= t_index
    cum = -rate * dot(step, causal.astype(F32), precision=lax.Precision.HIGHEST)
    last = cum[:, TOK - 1 : TOK]
    loads["mask"].wait()
    mask = mask_ref[...].astype(F32)
    stack[...] = jnp.zeros((128, TOK), F32)
    stack[0:8] = cum - jnp.log(step)
    stack[8:16] = jnp.exp(cum)
    stack[16:24] = jnp.exp(last - cum) * step
    stack[24:32] = jnp.broadcast_to(mask, (8, TOK))
    columns = stack[...].T
    cols_ref[...] = columns
    loads["x"].wait()
    loads["dir"].wait()
    loads["skip"].wait()
    loads["base"].wait()
    loads["stretch"].wait()
    low_half = lax.broadcasted_iota(jnp.int32, (TOK, 128), 1) < HEADDIM
    overlap = []

    def prepare(pair):
        columns = cols_ref[...]
        span = slice(128 * pair, 128 * pair + 128)
        x_pair = x_ref[:, span]
        x_wide = x_pair.astype(F32)
        dy_wide = dir_ref[:, span].astype(F32) * columns[:, 24:25]
        dy_pair = dy_wide.astype(BF16)
        dir_ref[:, span] = dy_pair
        scaled = (x_wide * pair_columns(columns, 16, pair, low_half)).astype(BF16)
        xf_ref[:, span] = scaled
        xf_t[span] = scaled.T
        scaled = (dy_wide * pair_columns(columns, 8, pair, low_half)).astype(BF16)
        dyg_ref[:, span] = scaled
        dyg_t[span] = scaled.T
        overlap.append(jnp.sum(x_wide * dy_wide, axis=0, keepdims=True))
        for h in (2 * pair, 2 * pair + 1):
            half = slice(HEADDIM * (h % 2), HEADDIM * (h % 2) + HEADDIM)
            gap = jnp.where(causal, cum[h : h + 1, :] - columns[:, h : h + 1], -1e30)
            factor = jnp.exp(gap)
            factors[h] = factor
            moves[h] = dot(x_pair[:, half], dy_pair[:, half], ((1,), (1,))) * factor
        skip_pair = jnp.where(low_half, skip_ref[2 * pair], skip_ref[2 * pair + 1])
        gx_ref[:, span] = skip_pair * dy_wide

    def forward_low(dz):
        where = (x, from_z(dz), c, low)
        arrive(buf, where, ("az", dz))
        for dx in far_x:
            send(buf, where, "plane", ("ax", dz), to_x(dx))
        send(buf, where, "mate", "mate", mate)

    def forward_high(dx):
        where = (from_x(dx), z, c, high)
        arrive(buf, where, ("bx", dx))
        for dz in far_z:
            send(buf, where, "plane", ("bz", dz), to_z(dz))
        send(buf, where, "mate", "mate", mate)

    def take_low(dz):
        zz = from_z(dz)
        arrive(buf, (pl.ds(0, NX - 1), zz, c, low), ("ax", dz))
        for dx in near_x:
            send(buf, (from_x(dx), zz, c, low), "mate", "mate", mate)

    def take_high(dz):
        where = (every, from_z(dz), c, high)
        arrive(buf, where, ("bz", dz))
        send(buf, where, "mate", "mate", mate)

    def turn(group):
        if group == 0:
            loads["hid"].wait()
        for j in range(4 * group, 4 * group + 4):
            span = slice(NC * DEPTH * j, NC * DEPTH * (j + 1))
            hid_t[span] = hid[:, span].T

    prepare(0)
    for dz in (1, 7):
        forward_low(dz)
    for dx in (1, 3):
        forward_high(dx)
    prepare(1)
    for dz in (2, 6):
        forward_low(dz)
    forward_high(2)
    prepare(2)
    for dz in (3, 5, 4):
        forward_low(dz)
    arrive(dec, (x, pl.ds(0, NZ - 1), c), "dz")
    for dx in near_x:
        send(dec, (x, every, c), "dx", "dx", to_x(dx))
    prepare(3)
    for group in range(5):
        turn(group)
    take_low(0)
    for dz in (1, 7):
        take_low(dz)
    for dz in (2, 6):
        take_low(dz)
    for dz in (1, 7, 2, 6):
        take_high(dz)
    for group in range(5, 8):
        turn(group)
    arrive(dec, (pl.ds(0, NX - 1), every, c), "dx")
    send(dec, (every, every, c), "dm", "dm", mate)
    for dz in (3, 5, 4):
        take_low(dz)
        take_high(dz)

    other = 1 - c
    arrive(buf, (every, every, other), "mate")
    span = MODEL // NX
    sums = jnp.zeros((TOK, COLS), F32)
    for k in range(NX):
        sums = sums + dot(hid[:, k * span : (k + 1) * span], buf[k].reshape(span, COLS))
    bc = sums.astype(BF16)
    b_in, c_in = bc[:, :NSTATE], bc[:, NSTATE:]
    lg[0] = dot(xf_t[...], b_in).reshape(2, WIDE // 2, NSTATE)
    lg[1] = dot(dyg_t[...], c_in).reshape(2, WIDE // 2, NSTATE)
    send(lg, (every, other), "lg", "l1", mate, mate_lg)
    send(lg, (every, c), "lg", "l2", mate, mate_lg)

    starts = sequence_starts(stretch_ref)
    arrive(dec, (every, every, other), "dm")
    row0, row1 = jnp.exp(dec[x, z, 0]), jnp.exp(dec[x, z, 1])
    lane1 = lax.broadcasted_iota(jnp.int32, (1, 128), 1)

    def pick(row, h):
        return jnp.sum(jnp.where(lane1 == h, row, 0.0), axis=1, keepdims=True)

    keep0, keep1 = keep_of(2 * chip, starts), keep_of(2 * chip + 1, starts)
    next1 = jnp.where(2 * chip + 2 == NCTX, 0.0, keep_of(2 * chip + 2, starts))
    first = c == 0
    arrive(mate_lg, (every, c), "l1")
    met = jnp.zeros((HEADDIM, 128), F32)
    chip_l, chip_g = [], []
    for hh in range(HEADS // 2):
        span = slice(HEADDIM * hh, HEADDIM * hh + HEADDIM)
        mine_l, mine_g = lg[0, c, span], lg[1, c, span]
        mate_l, mate_g = mate_lg[0, c, span], mate_lg[1, c, span]
        l0, l1 = jnp.where(first, mine_l, mate_l), jnp.where(first, mate_l, mine_l)
        g0, g1 = jnp.where(first, mine_g, mate_g), jnp.where(first, mate_g, mine_g)
        h = 4 * c + hh
        chip_l.append(pick(row1, h) * keep1 * l0 + l1)
        chip_g.append(pick(row0, h) * keep1 * g1 + g0)
        met = met + l0 * g1
    msg[...] = jnp.concatenate(
        [
            jnp.concatenate(chip_l, axis=0).reshape(CHIPS, 8, 128),
            jnp.concatenate(chip_g, axis=0).reshape(CHIPS, 8, 128),
        ],
        axis=1,
    ).astype(BF16)

    def exchange(source, target, phase):
        for dx, dz in FAR_FIRST:
            to = ((x + dx) % NX) * NZ + (z + dz) % NZ
            pltpu.make_async_remote_copy(
                source.at[to],
                target.at[chip],
                send_sem.at[phase],
                recv_sem.at[phase],
                device_id=(to * 2 + c, head),
                device_id_type=MESH,
            ).start()

    def settle(target, sem):
        rest = target.at[pl.ds(0, CHIPS - 1)]
        pltpu.make_async_copy(rest, rest, sem).wait()

    exchange(msg, got, 0)
    got[chip] = msg[chip]

    scores = dot(b_in, c_in, ((1,), (1,)))
    grad_scores = jnp.zeros((TOK, TOK), F32)
    back = jnp.zeros((TOK, 128), F32)
    lane128 = lax.broadcasted_iota(jnp.int32, (TOK, 128), 1)
    for pair in range(HEADS // 2):
        span = slice(128 * pair, 128 * pair + 128)
        within = []
        for h in (2 * pair, 2 * pair + 1):
            moved = moves[h]
            grad_scores = grad_scores + moved
            spent = moved * scores
            drow[h : h + 1] = jnp.sum(spent, axis=0, keepdims=True)
            back = jnp.where(lane128 == h, jnp.sum(spent, axis=1, keepdims=True), back)
            dy_h = dir_ref[:, HEADDIM * h : HEADDIM * h + HEADDIM]
            within.append(dot((scores * factors[h]).astype(BF16), dy_h))
        gx_ref[:, span] = gx_ref[:, span] + jnp.concatenate(within, axis=1)
    dcol[...] = back.T[0:8]
    grad_bf = grad_scores.astype(BF16)
    gcols_ref[:, :NSTATE] = dot(grad_bf, c_in)
    gcols_ref[:, NSTATE:] = dot(grad_bf, b_in, ((0,), (0,)))

    wide_row = lax.broadcasted_iota(jnp.int32, (WIDE, 128), 0) // HEADDIM
    wide_lane = lax.broadcasted_iota(jnp.int32, (WIDE, 128), 1)
    overlap_row = jnp.broadcast_to(jnp.concatenate(overlap, axis=1), (8, WIDE))
    overlap_head = dot(overlap_row, ((wide_row == wide_lane) | (wide_row == wide_lane - HEADS)).astype(F32), precision=lax.Precision.HIGHEST)
    skip_grads = overlap_head[1:2]
    skip_row = jnp.zeros((1, 128), F32)
    for h in range(HEADS):
        skip_row = jnp.where(lane1 == h, skip_ref[h], skip_row)
    pieces = jnp.sum(grad_scores * scores, axis=0, keepdims=True)
    pieces = pieces + jnp.where(head == 0, 1.0, 0.0) * mask * base_ref[...]
    own = pieces[:, :128] + pieces[:, 128:] + overlap_head[0:1] * skip_row
    own = jnp.sum(own, axis=1, keepdims=True)
    pair_sum = keep1 * jnp.sum(jnp.sum(met, axis=0, keepdims=True), axis=1, keepdims=True)
    mine = jnp.where(lane1 == seq_of(index, starts), own, 0.0)
    mine = mine + jnp.where(lane1 == seq_of(2 * chip + 1, starts), pair_sum, 0.0)

    chips = lax.broadcasted_iota(jnp.int32, (CHIPS, 128), 0)
    lane32 = lax.broadcasted_iota(jnp.int32, (CHIPS, 128), 1)
    my_head = 4 * c + chip // 8

    def decays(core):
        table = jnp.concatenate([dec[m // NZ, m % NZ, core] for m in range(CHIPS)], axis=0)
        return jnp.exp(jnp.sum(jnp.where(lane32 == my_head, table, 0.0), axis=1, keepdims=True))

    both = decays(0) * decays(1) * keep_of(2 * chips + 1, starts)
    enters = keep_of(2 * chips, starts)
    tab[0] = both * enters
    tab[1] = both * jnp.where(chips == CHIPS - 1, 0.0, keep_of(2 * chips + 2, starts))

    settle(got, recv_sem.at[0])
    wide[...] = got[...].astype(F32)

    def advance(b, carry):
        state, grad = carry
        r = CHIPS - 1 - b
        swept[b, 0:8] = state
        swept[r, 8:16] = grad
        state = state * tab[0, pl.ds(b, 1)] + wide[b, 0:8]
        grad = grad * tab[1, pl.ds(r, 1)] + wide[r, 8:16]
        return state, grad

    zero = jnp.zeros((8, 128), F32)
    lax.fori_loop(0, CHIPS, advance, (zero, zero))
    met = jnp.sum(swept[:, 0:8] * wide[:, 8:16], axis=1) * enters
    met = jnp.sum(met, axis=1, keepdims=True)
    seqs = seq_of(2 * chips, starts)
    mine = mine + jnp.sum(jnp.where(lane32 == seqs, met, 0.0), axis=0, keepdims=True)
    part[0] = mine

    for k, (dx, dz) in enumerate(FAR_FIRST):
        to = ((x + dx) % NX) * NZ + (z + dz) % NZ
        pltpu.make_async_remote_copy(
            part.at[0],
            near.at[k + 1],
            gs.at[0],
            gr.at[0],
            device_id=(to * 2 + c, head),
            device_id_type=MESH,
        ).start()
    near[0] = mine
    reply[...] = swept[...].astype(BF16)
    exchange(reply, states.at[c], 1)
    states[c, chip] = reply[chip]

    def settle_few(target, sem, count):
        rest = target.at[pl.ds(1, count)]
        pltpu.make_async_copy(rest, rest, sem).wait()

    settle_few(near, gr.at[0], CHIPS - 1)
    gathered = jnp.sum(near[...], axis=0)
    part[1] = gathered

    for k in HEADS_FAR_FIRST:
        pltpu.make_async_remote_copy(
            part.at[1],
            across.at[k],
            gs.at[1],
            gr.at[1],
            device_id=(chip * 2 + (c + k) % 2, (head + k // 2) % NHEAD),
            device_id_type=MESH,
        ).start()
    across[0] = gathered

    settle(states.at[c], recv_sem.at[1])
    send(states, (c,), "st", "st", mate)
    arrive(mate_lg, (every, other), "l2")

    def spaced(row):
        return jnp.concatenate(
            [jnp.broadcast_to(pick(row, h), (HEADDIM, 128)) for h in range(HEADS)], axis=0
        )

    lead = jnp.where(first, keep0, keep0 * keep1 * spaced(row0))
    lead_mate = jnp.where(first, 0.0, keep1)
    trail = jnp.where(first, next1 * keep1 * spaced(row1), next1)
    trail_mate = jnp.where(first, keep1, 0.0)
    arrive(states, (other,), "st")
    states_f = states[...].astype(F32)
    state_in = lead * states_f[:, :, 0:8].reshape(WIDE, NSTATE)
    state_in = state_in + lead_mate * mate_lg[0].reshape(WIDE, NSTATE)
    grad_state = trail * states_f[:, :, 8:16].reshape(WIDE, NSTATE)
    grad_state = grad_state + trail_mate * mate_lg[1].reshape(WIDE, NSTATE)

    state_bf, gstate_bf = state_in.astype(BF16), grad_state.astype(BF16)
    grads = jnp.concatenate(
        [
            gcols_ref[:, :NSTATE] + dot(xf_ref[...], gstate_bf),
            gcols_ref[:, NSTATE:] + dot(dyg_ref[...], state_bf),
        ],
        axis=1,
    ).astype(BF16)

    def token_grads():
        columns = cols_ref[...]
        pick_half = lanes8 // HEADDIM
        nt = ((1,), (1,))
        carried = jnp.zeros((8, TOK), F32)
        kept = jnp.zeros((8, TOK), F32)
        for pair in range(HEADS // 2):
            span = slice(128 * pair, 128 * pair + 128)
            picks = (rows8 == 2 * pair + pick_half).astype(BF16)
            top, rest = halves(dot(c_in, state_bf[span], nt) * dyg_ref[:, span].astype(F32))
            carried = carried + dot(picks, top, nt) + dot(picks, rest, nt)
            pulled = dot(b_in, gstate_bf[span], nt) * pair_columns(columns, 16, pair, low_half)
            top, rest = halves(pulled * x_ref[:, span].astype(F32))
            kept = kept + dot(picks, top, nt) + dot(picks, rest, nt)
            gx_ref[:, span] = gx_ref[:, span] + pulled
        grad_decay = jnp.sum(
            jnp.sum((state_in * grad_state).reshape(HEADS, HEADDIM, NSTATE), axis=1), axis=1, keepdims=True
        )
        end = jnp.sum(kept, axis=1, keepdims=True) + grad_decay * jnp.exp(last)
        token = lax.broadcasted_iota(jnp.int32, (8, TOK), 1)
        grad_cum = drow[...] - dcol[...] + carried - kept + jnp.where(token == TOK - 1, end, 0.0)
        tail = dot(grad_cum, (s_index >= t_index).astype(F32), precision=lax.Precision.HIGHEST)
        gstep_ref[...] = (dcol[...] + kept) / step - rate * tail
        grad_rate = -jnp.sum(step * tail, axis=1, keepdims=True)
        rate_row = jnp.sum(jnp.where(lanes8 == rows8, grad_rate, 0.0), axis=0, keepdims=True)
        few[0] = jnp.where(lane1 < HEADS, rate_row, skip_grads)

    order = (4, 3, 5, 2, 6, 1, 7, 0)

    def multiply(k):
        zz = (z + order[k]) % NZ
        for dx in range(NX):
            first_column = (((x + dx) % NX) * NZ + zz) * (NC * DEPTH)
            chunk = hid_t[pl.ds(pl.multiple_of(first_column, NC * DEPTH), NC * DEPTH)]
            prod[k, dx] = dot(chunk, grads).reshape(NC, DEPTH, COLS)
            mate_out[k, dx] = prod[k, dx, other].astype(BF16)
        send(mate_out, (k,), "m", ("m", k), mate, mate_in)

    def scale_of(block, seq_sums):
        one, two, three = starts
        chosen = jnp.where(block >= two, 2, 0)
        signed = jnp.where(lane1 == chosen, seq_sums, 0.0) - jnp.where(lane1 == chosen + 1, seq_sums, 0.0)
        margin = jnp.sum(signed, axis=1, keepdims=True)
        coef = 1.0 / (1.0 + jnp.exp(-hinge_sharp * (hinge_margin - margin)))
        rejected = ((block >= one) & (block < two)) | (block >= three)
        return jnp.where(rejected, coef, -coef)

    def combine(k):
        dz = order[k]
        arrive(mate_in, (k,), ("m", k))
        for dx in (2, 1, 3):
            both = prod[k, dx, c] * scale + mate_in[k, dx].astype(F32) * scale_mate
            a_out[k, dx - 1] = both[:PART].astype(BF16)
            send(a_out, (k, dx - 1), "a", ("a", k), to_x(dx), a_in)
            prod[k, dx, c, PART:] = both[PART:]
        both = prod[k, 0, c] * scale + mate_in[k, 0].astype(F32) * scale_mate
        a_own[k] = both[:PART]
        prod[k, 0, c, PART:] = both[PART:]
        if dz:
            b_out[k] = prod[k, :, c, PART:].astype(BF16)
            send(b_out, (k,), "b", "b", to_z(dz), bz_in)

    def pass_on(k):
        dz = order[k]
        arrive(a_in, (k,), ("a", k))
        a_own[k] = a_own[k] + jnp.sum(a_in[k].astype(F32), axis=0)
        if dz:
            a2_out[k] = a_own[k].astype(BF16)
            send(a2_out, (k,), "a2", "a2", to_z(dz), a2_in)

    for k in range(AHEAD):
        multiply(k)
    token_grads()
    settle_few(across, gr.at[1], 2 * NHEAD - 1)
    seq_sums = jnp.sum(across[...], axis=0)
    scale, scale_mate = scale_of(index, seq_sums), scale_of(index + 1 - 2 * c, seq_sums)
    few[0] = few[0] * scale
    move(few.at[0], few_c, "fc", "fc", mate)
    for k in range(NZ):
        combine(k)
        if k == 1:
            arrive(few_c, (every,), "fc")
            few[1] = few[0] + few_c[...]
            for j, (dx, dz) in enumerate(FAR_FIRST):
                move(few.at[1], few_all.at[j], "fz", "fz", at(x + dx, z + dz, c, head))
        if k + AHEAD < NZ:
            multiply(k + AHEAD)

    gx_bf[...] = (gx_ref[...] * scale).astype(BF16)
    gstep_ref[...] = gstep_ref[...] * scale
    stores = [
        pltpu.make_async_copy(gx_bf, grad_x_out, load_sem.at[0]),
        pltpu.make_async_copy(gstep_ref, grad_step_out, load_sem.at[1]),
    ]
    for store in stores:
        store.start()
    pass_on(0)
    for k in range(1, 4):
        pass_on(k)
    pass_on(4)
    b_sum = prod[NZ - 1, :, c, PART:]
    arrive(bz_in, (every,), "b")
    for k in range(NZ - 1):
        b_sum = b_sum + bz_in[k].astype(F32)
    for dx in (2, 1, 3):
        b2_out[dx - 1] = b_sum[dx].astype(BF16)
        send(b2_out, (dx - 1,), "b2", "b2", to_x(dx), b2_in)
    for k in range(5, NZ):
        pass_on(k)
    arrive(b2_in, (every,), "b2")
    gw_ref[PART:] = b_sum[0] + jnp.sum(b2_in[...].astype(F32), axis=0)
    a_sum = a_own[NZ - 1]
    arrive(few_all, (every,), "fz")
    small = few[1] + jnp.sum(few_all[...], axis=0)
    for h in range(HEADS):
        rate_ref[h] = small[0, h]
        skip_ref[h] = small[0, HEADS + h]
    stores.append(pltpu.make_async_copy(rate_ref, rate_out, load_sem.at[2]))
    stores.append(pltpu.make_async_copy(skip_ref, skip_out, load_sem.at[4]))
    stores[-2].start()
    stores[-1].start()
    arrive(a2_in, (every,), "a2")
    for k in range(NZ - 1):
        a_sum = a_sum + a2_in[k].astype(F32)
    gw_ref[:PART] = a_sum
    stores.append(pltpu.make_async_copy(gw_ref, grad_w_out, load_sem.at[3]))
    stores[-1].start()

    drain("plane", moves.at[pl.ds(0, NZ // 2), pl.ds(0, TOK - 8)])
    drain("mate", buf.at[:, :, c])
    drain("dz", dec.at[x, pl.ds(0, NZ - 1), c])
    drain("dx", dec.at[pl.ds(0, NX - 1), :, c])
    drain("dm", dec.at[:, :, c])
    drain("lg", lg)
    drain("st", states.at[c])
    drain("m", mate_out)
    drain("a", a_out)
    drain("b", b_out)
    drain("a2", a2_out)
    drain("b2", b2_out)
    drain("fc", few.at[0])
    drain("fz", few_all)
    assert not sent
    settle(msg, send_sem.at[0])
    settle(reply, send_sem.at[1])
    settle_few(near, gs.at[0], CHIPS - 1)
    settle_few(across, gs.at[1], 2 * NHEAD - 1)
    for store in stores:
        store.wait()


def whole(hidden, w_bc, x_act, logp_dir, step_size, rate, skip, mask, base, stretches):
    shape = jax.ShapeDtypeStruct
    rest = DEPTH - PART
    return pl.pallas_call(
        whole_kernel,
        name="whole",
        out_shape=(
            shape((TOK, WIDE), BF16),
            shape((8, TOK), F32),
            shape((HEADS,), F32),
            shape((HEADS,), F32),
            shape((DEPTH, COLS), F32),
        ),
        in_specs=[pl.BlockSpec(memory_space=SPACE)] * 10,
        out_specs=tuple([pl.BlockSpec(memory_space=SPACE)] * 5),
        scratch_shapes=[
            pltpu.VMEM((TOK, MODEL), BF16),
            pltpu.VMEM((TOK, WIDE), BF16),
            pltpu.VMEM((TOK, WIDE), BF16),
            pltpu.VMEM((8, TOK), F32),
            pltpu.SMEM((8,), F32),
            pltpu.SMEM((8,), F32),
            pltpu.VMEM((1, TOK), jnp.int32),
            pltpu.VMEM((1, TOK), F32),
            pltpu.SMEM((4,), jnp.int32),
            pltpu.VMEM((NX, NZ, NC, DEPTH, COLS), BF16),
            pltpu.VMEM((NX, NZ, NC, 1, 128), F32),
            pltpu.VMEM((HEADS, TOK, TOK), F32),
            pltpu.VMEM((HEADS, TOK, TOK), F32),
            pltpu.VMEM((128, TOK), F32),
            pltpu.VMEM((TOK, 128), F32),
            pltpu.VMEM((TOK, WIDE), BF16),
            pltpu.VMEM((TOK, WIDE), BF16),
            pltpu.VMEM((8, TOK), F32),
            pltpu.VMEM((8, TOK), F32),
            pltpu.VMEM((2, 2, WIDE // 2, NSTATE), F32),
            pltpu.VMEM((2, 2, WIDE // 2, NSTATE), F32),
            pltpu.VMEM((CHIPS, 16, 128), BF16),
            pltpu.VMEM((CHIPS, 16, 128), BF16),
            pltpu.VMEM((CHIPS, 16, 128), F32),
            pltpu.VMEM((CHIPS, 16, 128), F32),
            pltpu.VMEM((CHIPS, 16, 128), BF16),
            pltpu.VMEM((2, CHIPS, 16, 128), BF16),
            pltpu.VMEM((2, CHIPS, 128), F32),
            pltpu.VMEM((2, 1, 128), F32),
            pltpu.VMEM((CHIPS, 1, 128), F32),
            pltpu.VMEM((2 * NHEAD, 1, 128), F32),
            pltpu.VMEM((MODEL, TOK), BF16),
            pltpu.VMEM((WIDE, TOK), BF16),
            pltpu.VMEM((WIDE, TOK), BF16),
            pltpu.VMEM((TOK, WIDE), F32),
            pltpu.VMEM((TOK, COLS), F32),
            pltpu.VMEM((TOK, WIDE), BF16),
            pltpu.VMEM((8, TOK), F32),
            pltpu.VMEM((DEPTH, COLS), F32),
            pltpu.VMEM((NZ, NX, NC, DEPTH, COLS), F32),
            pltpu.VMEM((NZ, NX, DEPTH, COLS), BF16),
            pltpu.VMEM((NZ, NX, DEPTH, COLS), BF16),
            pltpu.VMEM((NZ, NX - 1, PART, COLS), BF16),
            pltpu.VMEM((NZ, PART, COLS), F32),
            pltpu.VMEM((NZ, NX - 1, PART, COLS), BF16),
            pltpu.VMEM((NZ - 1, PART, COLS), BF16),
            pltpu.VMEM((NZ - 1, PART, COLS), BF16),
            pltpu.VMEM((NZ - 1, NX, rest, COLS), BF16),
            pltpu.VMEM((NZ - 1, NX, rest, COLS), BF16),
            pltpu.VMEM((NX - 1, rest, COLS), BF16),
            pltpu.VMEM((NX - 1, rest, COLS), BF16),
            pltpu.VMEM((2, 1, 128), F32),
            pltpu.VMEM((1, 128), F32),
            pltpu.VMEM((CHIPS - 1, 1, 128), F32),
            pltpu.SemaphoreType.DMA((10,)),
            pltpu.SemaphoreType.DMA((2,)),
            pltpu.SemaphoreType.DMA((2,)),
            pltpu.SemaphoreType.DMA((14,)),
            pltpu.SemaphoreType.DMA((53,)),
            pltpu.SemaphoreType.DMA((2,)),
            pltpu.SemaphoreType.DMA((2,)),
        ],
        compiler_params=pltpu.CompilerParams(
            collective_id=0, has_side_effects=True, vmem_limit_bytes=VMEM_LIMIT
        ),
    )(hidden, w_bc, x_act, logp_dir, step_size, rate, skip, mask, base, stretches)


def finish_kernel(*refs):
    *ends, sems = refs
    count = len(ends) // 3
    sources, targets, holds = ends[:count], ends[count : 2 * count], ends[2 * count :]
    into = [pltpu.make_async_copy(sources[k], holds[k], sems.at[k]) for k in range(count)]
    back = [pltpu.make_async_copy(holds[k], targets[k], sems.at[count + k]) for k in range(count)]
    for copy in into:
        copy.start()
    for k in reversed(range(count)):
        into[k].wait()
        back[k].start()
    for copy in back:
        copy.wait()


def finish(*arrays):
    spec = pl.BlockSpec(memory_space=SPACE)
    return pl.pallas_call(
        finish_kernel,
        name="finish",
        out_shape=tuple(jax.ShapeDtypeStruct(array.shape, array.dtype) for array in arrays),
        in_specs=[spec] * len(arrays),
        out_specs=tuple([spec] * len(arrays)),
        scratch_shapes=[
            (pltpu.VMEM if array.ndim == 2 else pltpu.SMEM)(array.shape, array.dtype) for array in arrays
        ]
        + [pltpu.SemaphoreType.DMA((2 * len(arrays),))],
        compiler_params=pltpu.CompilerParams(vmem_limit_bytes=VMEM_LIMIT),
    )(*arrays)


def body(
    hidden, w_bc, x_act, step_size, decay_rate, skip_gain, logp_dir, base_logp, seq_stretches, resp_mask
):
    return finish(
        *whole(
            hidden, w_bc, x_act, logp_dir, step_size, decay_rate, skip_gain,
            resp_mask.reshape(1, TOK), base_logp.reshape(1, TOK), seq_stretches,
        )
    )


def solution(mesh):
    return jax.shard_map(
        body,
        mesh=mesh,
        in_specs=(
            P("ctx", None),
            P("ctx", "head"),
            P("ctx", "head"),
            P("head", "ctx"),
            P("head"),
            P("head"),
            P("ctx", "head"),
            P("ctx"),
            P(),
            P("ctx"),
        ),
        out_specs=(P("ctx", "head"), P("head", "ctx"), P("head"), P("head"), P("ctx", "head")),
        check_vma=False,
    )
```

```python
import functools

import jax
import jax.numpy as jnp
from jax import lax
from jax.experimental import pallas as pl
from jax.experimental.pallas import tpu as pltpu
from jax.sharding import PartitionSpec as P

HEADDIM = 64
NSTATE = 128
NX, NZ, NC = 4, 8, 2
NCTX = NX * NZ * NC
CHIPS = NX * NZ
NHEAD = 8
TOK = 256
HEADS = 8
WIDE = HEADS * HEADDIM
DEPTH = 64
COLS = 2 * NSTATE
MODEL = NCTX * DEPTH
PART = 48
AHEAD = 4

hinge_sharp = 0.005
hinge_margin = 10.0

FAR_FIRST = sorted(
    [(dx, dz) for dx in range(NX) for dz in range(NZ) if dx or dz],
    key=lambda step: -(min(step[0], NX - step[0]) + min(step[1], NZ - step[1])),
)

HEADS_FAR_FIRST = (8, 9, 6, 7, 10, 11, 4, 5, 12, 13, 2, 3, 14, 15, 1)

MESH = pl.DeviceIdType.MESH
F32 = jnp.float32
BF16 = jnp.bfloat16
VMEM_LIMIT = 64 << 20
SPACE = pltpu.HBM


def place():
    index = lax.axis_index("ctx")
    return index // 16, (index // 2) % 8, index % 2, lax.axis_index("head")


def at(x, z, c, head):
    return (((x % NX) * NZ + (z % NZ)) * NC + c, head)


def dot(left, right, dims=((1,), (0,)), precision=None):
    return lax.dot_general(left, right, (dims, ((), ())), precision=precision, preferred_element_type=F32)


def pair_columns(columns, base, pair, low_half):
    one, two = base + 2 * pair, base + 2 * pair + 1
    return jnp.where(low_half, columns[:, one : one + 1], columns[:, two : two + 1])


def sequence_starts(stretch_ref):
    one = stretch_ref[0]
    two = one + stretch_ref[1]
    return one, two, two + stretch_ref[2]


def halves(value):
    top = value.astype(BF16)
    return top, (value - top.astype(F32)).astype(BF16)


def keep_of(block, starts):
    begins = block == 0
    for start in starts:
        begins = begins | (block == start)
    return jnp.where(begins, 0.0, 1.0)


def seq_of(block, starts):
    return sum((block >= start).astype(jnp.int32) for start in starts)


def whole_kernel(
    hid_hbm, w_hbm, x_hbm, dir_hbm, step_hbm, rate_hbm, skip_hbm, mask_hbm, base_hbm, stretch_hbm,
    grad_x_out, grad_step_out, rate_out, skip_out, grad_w_out,
    hid, x_ref, dir_ref, step_ref, rate_ref, skip_ref, mask_ref, base_ref, stretch_ref,
    buf, dec, factors, moves, stack, cols_ref, xf_ref, dyg_ref, drow, dcol, lg, mate_lg, msg, got, wide,
    swept, reply, states, tab, part, near, across,
    hid_t, xf_t, dyg_t, gx_ref, gcols_ref, gx_bf, gstep_ref, gw_ref,
    prod, mate_out, mate_in, a_out, a_own, a_in, a2_out, a2_in, b_out, bz_in, b2_out, b2_in,
    few, few_c, few_all,
    load_sem, send_sem, recv_sem, ss, rs, gs, gr,
):
    index = lax.axis_index("ctx")
    x, z, c, head = place()
    chip = index // 2
    mate = at(x, z, 1 - c, head)
    every = slice(None)

    barrier = pltpu.get_barrier_semaphore()

    def hello(partner):
        pl.semaphore_signal(barrier, inc=1, device_id=partner, device_id_type=MESH)

    for dz in (4, 3, 5, 2, 6, 1, 7):
        hello(at(x, z + dz, c, head))
    for dx in (2, 1, 3):
        hello(at(x + dx, z, c, head))
    hello(mate)
    loads = {}
    for k, (name, source, target) in enumerate(
        (
            ("step", step_hbm, step_ref),
            ("rate", rate_hbm, rate_ref),
            ("w", w_hbm, buf.at[x, z, c]),
            ("mask", mask_hbm, mask_ref),
            ("x", x_hbm, x_ref),
            ("dir", dir_hbm, dir_ref),
            ("skip", skip_hbm, skip_ref),
            ("base", base_hbm, base_ref),
            ("stretch", stretch_hbm, stretch_ref),
            ("hid", hid_hbm, hid),
        )
    ):
        loads[name] = pltpu.make_async_copy(source, target, load_sem.at[k])
        loads[name].start()

    for k in range(2, 2 * NHEAD):
        hello((chip * 2 + (c + k) % 2, (head + k // 2) % NHEAD))
    loads["w"].wait()
    pl.semaphore_wait(barrier, NZ - 1 + NX - 1 + 2 * NHEAD - 1)

    sent, landed = {}, {}

    def slot(table, key):
        return table.setdefault(key, len(table))

    def move(source, target, out, key, partner):
        pltpu.make_async_remote_copy(
            source,
            target,
            ss.at[slot(sent, out)],
            rs.at[slot(landed, key)],
            device_id=partner,
            device_id_type=MESH,
        ).start()

    def send(ref, where, out, key, partner, into=None):
        move(ref.at[where], (ref if into is None else into).at[where], out, key, partner)

    def arrive(ref, where, key):
        piece = ref.at[where]
        pltpu.make_async_copy(piece, piece, rs.at[slot(landed, key)]).wait()

    def drain(out, piece):
        pltpu.make_async_copy(piece, piece, ss.at[sent.pop(out)]).wait()

    low, high = pl.ds(0, PART), pl.ds(PART, DEPTH - PART)
    near_z, near_x = (1, 7, 2, 6, 3, 5, 4), (1, 3, 2)
    far_z, far_x = (4, 3, 5, 2, 6, 1, 7), (2, 1, 3)

    def to_z(dz):
        return at(x, z + dz, c, head)

    def to_x(dx):
        return at(x + dx, z, c, head)

    def from_z(dz):
        return (z - dz) % NZ

    def from_x(dx):
        return (x - dx) % NX

    for dz in near_z:
        send(buf, (x, z, c, low), "plane", ("az", dz), to_z(dz))
    for dx in near_x:
        send(buf, (x, z, c, high), "plane", ("bx", dx), to_x(dx))
    for dx in near_x:
        send(buf, (x, z, c, low), "plane", ("ax", 0), to_x(dx))
    for dz in far_z:
        send(buf, (x, z, c, high), "plane", ("bz", dz), to_z(dz))
    send(buf, (x, z, c), "mate", "mate", mate)

    loads["step"].wait()
    loads["rate"].wait()
    rows8 = lax.broadcasted_iota(jnp.int32, (8, 128), 0)
    lanes8 = lax.broadcasted_iota(jnp.int32, (8, 128), 1)
    step = step_ref[...]
    row8 = lax.broadcasted_iota(jnp.int32, (8, TOK), 0)
    rate = jnp.zeros((8, TOK), F32)
    for h in range(HEADS):
        rate = jnp.where(row8 == h, rate_ref[h], rate)
    total = -rate[:, 0:1] * jnp.sum(step, axis=1, keepdims=True)
    dec[x, z, c] = jnp.sum(jnp.where(rows8 == lanes8, total, 0.0), axis=0, keepdims=True)
    for dz in near_z:
        send(dec, (x, z, c), "dz", "dz", to_z(dz))

    s_index = lax.broadcasted_iota(jnp.int32, (TOK, TOK), 0)
    t_index = lax.broadcasted_iota(jnp.int32, (TOK, TOK), 1)
    causal = s_index <= t_index
    cum = -rate * dot(step, causal.astype(F32), precision=lax.Precision.HIGHEST)
    last = cum[:, TOK - 1 : TOK]
    loads["mask"].wait()
    mask = mask_ref[...].astype(F32)
    stack[...] = jnp.zeros((128, TOK), F32)
    stack[0:8] = cum - jnp.log(step)
    stack[8:16] = jnp.exp(cum)
    stack[16:24] = jnp.exp(last - cum) * step
    stack[24:32] = jnp.broadcast_to(mask, (8, TOK))
    columns = stack[...].T
    cols_ref[...] = columns
    loads["x"].wait()
    loads["dir"].wait()
    loads["skip"].wait()
    loads["base"].wait()
    loads["stretch"].wait()
    low_half = lax.broadcasted_iota(jnp.int32, (TOK, 128), 1) < HEADDIM
    overlap = []

    def prepare(pair):
        columns = cols_ref[...]
        span = slice(128 * pair, 128 * pair + 128)
        x_pair = x_ref[:, span]
        x_wide = x_pair.astype(F32)
        dy_wide = dir_ref[:, span].astype(F32) * columns[:, 24:25]
        dy_pair = dy_wide.astype(BF16)
        dir_ref[:, span] = dy_pair
        scaled = (x_wide * pair_columns(columns, 16, pair, low_half)).astype(BF16)
        xf_ref[:, span] = scaled
        xf_t[span] = scaled.T
        scaled = (dy_wide * pair_columns(columns, 8, pair, low_half)).astype(BF16)
        dyg_ref[:, span] = scaled
        dyg_t[span] = scaled.T
        overlap.append(jnp.sum(x_wide * dy_wide, axis=0, keepdims=True))
        for h in (2 * pair, 2 * pair + 1):
            half = slice(HEADDIM * (h % 2), HEADDIM * (h % 2) + HEADDIM)
            gap = jnp.where(causal, cum[h : h + 1, :] - columns[:, h : h + 1], -1e30)
            factor = jnp.exp(gap)
            factors[h] = factor
            moves[h] = dot(x_pair[:, half], dy_pair[:, half], ((1,), (1,))) * factor
        skip_pair = jnp.where(low_half, skip_ref[2 * pair], skip_ref[2 * pair + 1])
        gx_ref[:, span] = skip_pair * dy_wide

    def forward_low(dz):
        where = (x, from_z(dz), c, low)
        arrive(buf, where, ("az", dz))
        for dx in far_x:
            send(buf, where, "plane", ("ax", dz), to_x(dx))
        send(buf, where, "mate", "mate", mate)

    def forward_high(dx):
        where = (from_x(dx), z, c, high)
        arrive(buf, where, ("bx", dx))
        for dz in far_z:
            send(buf, where, "plane", ("bz", dz), to_z(dz))
        send(buf, where, "mate", "mate", mate)

    def take_low(dz):
        zz = from_z(dz)
        arrive(buf, (pl.ds(0, NX - 1), zz, c, low), ("ax", dz))
        for dx in near_x:
            send(buf, (from_x(dx), zz, c, low), "mate", "mate", mate)

    def take_high(dz):
        where = (every, from_z(dz), c, high)
        arrive(buf, where, ("bz", dz))
        send(buf, where, "mate", "mate", mate)

    def turn(group):
        if group == 0:
            loads["hid"].wait()
        for j in range(4 * group, 4 * group + 4):
            span = slice(NC * DEPTH * j, NC * DEPTH * (j + 1))
            hid_t[span] = hid[:, span].T

    prepare(0)
    for dz in (1, 7):
        forward_low(dz)
    for dx in (1, 3):
        forward_high(dx)
    prepare(1)
    for dz in (2, 6):
        forward_low(dz)
    forward_high(2)
    prepare(2)
    for dz in (3, 5, 4):
        forward_low(dz)
    arrive(dec, (x, pl.ds(0, NZ - 1), c), "dz")
    for dx in near_x:
        send(dec, (x, every, c), "dx", "dx", to_x(dx))
    prepare(3)
    for group in range(5):
        turn(group)
    take_low(0)
    for dz in (1, 7):
        take_low(dz)
    for dz in (2, 6):
        take_low(dz)
    for dz in (1, 7, 2, 6):
        take_high(dz)
    for group in range(5, 8):
        turn(group)
    arrive(dec, (pl.ds(0, NX - 1), every, c), "dx")
    send(dec, (every, every, c), "dm", "dm", mate)
    for dz in (3, 5, 4):
        take_low(dz)
        take_high(dz)

    other = 1 - c
    arrive(buf, (every, every, other), "mate")
    span = MODEL // NX
    sums = jnp.zeros((TOK, COLS), F32)
    for k in range(NX):
        sums = sums + dot(hid[:, k * span : (k + 1) * span], buf[k].reshape(span, COLS))
    bc = sums.astype(BF16)
    b_in, c_in = bc[:, :NSTATE], bc[:, NSTATE:]
    lg[0] = dot(xf_t[...], b_in).reshape(2, WIDE // 2, NSTATE)
    lg[1] = dot(dyg_t[...], c_in).reshape(2, WIDE // 2, NSTATE)
    send(lg, (every, other), "lg", "l1", mate, mate_lg)
    send(lg, (every, c), "lg", "l2", mate, mate_lg)

    starts = sequence_starts(stretch_ref)
    arrive(dec, (every, every, other), "dm")
    row0, row1 = jnp.exp(dec[x, z, 0]), jnp.exp(dec[x, z, 1])
    lane1 = lax.broadcasted_iota(jnp.int32, (1, 128), 1)

    def pick(row, h):
        return jnp.sum(jnp.where(lane1 == h, row, 0.0), axis=1, keepdims=True)

    keep0, keep1 = keep_of(2 * chip, starts), keep_of(2 * chip + 1, starts)
    next1 = jnp.where(2 * chip + 2 == NCTX, 0.0, keep_of(2 * chip + 2, starts))
    first = c == 0
    arrive(mate_lg, (every, c), "l1")
    met = jnp.zeros((HEADDIM, 128), F32)
    chip_l, chip_g = [], []
    for hh in range(HEADS // 2):
        span = slice(HEADDIM * hh, HEADDIM * hh + HEADDIM)
        mine_l, mine_g = lg[0, c, span], lg[1, c, span]
        mate_l, mate_g = mate_lg[0, c, span], mate_lg[1, c, span]
        l0, l1 = jnp.where(first, mine_l, mate_l), jnp.where(first, mate_l, mine_l)
        g0, g1 = jnp.where(first, mine_g, mate_g), jnp.where(first, mate_g, mine_g)
        h = 4 * c + hh
        chip_l.append(pick(row1, h) * keep1 * l0 + l1)
        chip_g.append(pick(row0, h) * keep1 * g1 + g0)
        met = met + l0 * g1
    msg[...] = jnp.concatenate(
        [
            jnp.concatenate(chip_l, axis=0).reshape(CHIPS, 8, 128),
            jnp.concatenate(chip_g, axis=0).reshape(CHIPS, 8, 128),
        ],
        axis=1,
    ).astype(BF16)

    def exchange(source, target, phase):
        for dx, dz in FAR_FIRST:
            to = ((x + dx) % NX) * NZ + (z + dz) % NZ
            pltpu.make_async_remote_copy(
                source.at[to],
                target.at[chip],
                send_sem.at[phase],
                recv_sem.at[phase],
                device_id=(to * 2 + c, head),
                device_id_type=MESH,
            ).start()

    def settle(target, sem):
        rest = target.at[pl.ds(0, CHIPS - 1)]
        pltpu.make_async_copy(rest, rest, sem).wait()

    exchange(msg, got, 0)
    got[chip] = msg[chip]

    scores = dot(b_in, c_in, ((1,), (1,)))
    grad_scores = jnp.zeros((TOK, TOK), F32)
    back = jnp.zeros((TOK, 128), F32)
    lane128 = lax.broadcasted_iota(jnp.int32, (TOK, 128), 1)
    for pair in range(HEADS // 2):
        span = slice(128 * pair, 128 * pair + 128)
        within = []
        for h in (2 * pair, 2 * pair + 1):
            moved = moves[h]
            grad_scores = grad_scores + moved
            spent = moved * scores
            drow[h : h + 1] = jnp.sum(spent, axis=0, keepdims=True)
            back = jnp.where(lane128 == h, jnp.sum(spent, axis=1, keepdims=True), back)
            dy_h = dir_ref[:, HEADDIM * h : HEADDIM * h + HEADDIM]
            within.append(dot((scores * factors[h]).astype(BF16), dy_h))
        gx_ref[:, span] = gx_ref[:, span] + jnp.concatenate(within, axis=1)
    dcol[...] = back.T[0:8]
    grad_bf = grad_scores.astype(BF16)
    gcols_ref[:, :NSTATE] = dot(grad_bf, c_in)
    gcols_ref[:, NSTATE:] = dot(grad_bf, b_in, ((0,), (0,)))

    wide_row = lax.broadcasted_iota(jnp.int32, (WIDE, 128), 0) // HEADDIM
    wide_lane = lax.broadcasted_iota(jnp.int32, (WIDE, 128), 1)
    overlap_row = jnp.broadcast_to(jnp.concatenate(overlap, axis=1), (8, WIDE))
    overlap_head = dot(overlap_row, ((wide_row == wide_lane) | (wide_row == wide_lane - HEADS)).astype(F32), precision=lax.Precision.HIGHEST)
    skip_grads = overlap_head[1:2]
    skip_row = jnp.zeros((1, 128), F32)
    for h in range(HEADS):
        skip_row = jnp.where(lane1 == h, skip_ref[h], skip_row)
    pieces = jnp.sum(grad_scores * scores, axis=0, keepdims=True)
    pieces = pieces + jnp.where(head == 0, 1.0, 0.0) * mask * base_ref[...]
    own = pieces[:, :128] + pieces[:, 128:] + overlap_head[0:1] * skip_row
    own = jnp.sum(own, axis=1, keepdims=True)
    pair_sum = keep1 * jnp.sum(jnp.sum(met, axis=0, keepdims=True), axis=1, keepdims=True)
    mine = jnp.where(lane1 == seq_of(index, starts), own, 0.0)
    mine = mine + jnp.where(lane1 == seq_of(2 * chip + 1, starts), pair_sum, 0.0)

    chips = lax.broadcasted_iota(jnp.int32, (CHIPS, 128), 0)
    lane32 = lax.broadcasted_iota(jnp.int32, (CHIPS, 128), 1)
    my_head = 4 * c + chip // 8

    def decays(core):
        table = jnp.concatenate([dec[m // NZ, m % NZ, core] for m in range(CHIPS)], axis=0)
        return jnp.exp(jnp.sum(jnp.where(lane32 == my_head, table, 0.0), axis=1, keepdims=True))

    both = decays(0) * decays(1) * keep_of(2 * chips + 1, starts)
    enters = keep_of(2 * chips, starts)
    tab[0] = both * enters
    tab[1] = both * jnp.where(chips == CHIPS - 1, 0.0, keep_of(2 * chips + 2, starts))

    settle(got, recv_sem.at[0])
    wide[...] = got[...].astype(F32)

    def advance(b, carry):
        state, grad = carry
        r = CHIPS - 1 - b
        swept[b, 0:8] = state
        swept[r, 8:16] = grad
        state = state * tab[0, pl.ds(b, 1)] + wide[b, 0:8]
        grad = grad * tab[1, pl.ds(r, 1)] + wide[r, 8:16]
        return state, grad

    zero = jnp.zeros((8, 128), F32)
    lax.fori_loop(0, CHIPS, advance, (zero, zero))
    met = jnp.sum(swept[:, 0:8] * wide[:, 8:16], axis=1) * enters
    met = jnp.sum(met, axis=1, keepdims=True)
    seqs = seq_of(2 * chips, starts)
    mine = mine + jnp.sum(jnp.where(lane32 == seqs, met, 0.0), axis=0, keepdims=True)
    part[0] = mine

    for k, (dx, dz) in enumerate(FAR_FIRST):
        to = ((x + dx) % NX) * NZ + (z + dz) % NZ
        pltpu.make_async_remote_copy(
            part.at[0],
            near.at[k + 1],
            gs.at[0],
            gr.at[0],
            device_id=(to * 2 + c, head),
            device_id_type=MESH,
        ).start()
    near[0] = mine
    reply[...] = swept[...].astype(BF16)
    exchange(reply, states.at[c], 1)
    states[c, chip] = reply[chip]

    def settle_few(target, sem, count):
        rest = target.at[pl.ds(1, count)]
        pltpu.make_async_copy(rest, rest, sem).wait()

    settle_few(near, gr.at[0], CHIPS - 1)
    gathered = jnp.sum(near[...], axis=0)
    part[1] = gathered

    for k in HEADS_FAR_FIRST:
        pltpu.make_async_remote_copy(
            part.at[1],
            across.at[k],
            gs.at[1],
            gr.at[1],
            device_id=(chip * 2 + (c + k) % 2, (head + k // 2) % NHEAD),
            device_id_type=MESH,
        ).start()
    across[0] = gathered

    settle(states.at[c], recv_sem.at[1])
    send(states, (c,), "st", "st", mate)
    arrive(mate_lg, (every, other), "l2")

    def spaced(row):
        return jnp.concatenate(
            [jnp.broadcast_to(pick(row, h), (HEADDIM, 128)) for h in range(HEADS)], axis=0
        )

    lead = jnp.where(first, keep0, keep0 * keep1 * spaced(row0))
    lead_mate = jnp.where(first, 0.0, keep1)
    trail = jnp.where(first, next1 * keep1 * spaced(row1), next1)
    trail_mate = jnp.where(first, keep1, 0.0)
    arrive(states, (other,), "st")
    states_f = states[...].astype(F32)
    state_in = lead * states_f[:, :, 0:8].reshape(WIDE, NSTATE)
    state_in = state_in + lead_mate * mate_lg[0].reshape(WIDE, NSTATE)
    grad_state = trail * states_f[:, :, 8:16].reshape(WIDE, NSTATE)
    grad_state = grad_state + trail_mate * mate_lg[1].reshape(WIDE, NSTATE)

    state_bf, gstate_bf = state_in.astype(BF16), grad_state.astype(BF16)
    grads = jnp.concatenate(
        [
            gcols_ref[:, :NSTATE] + dot(xf_ref[...], gstate_bf),
            gcols_ref[:, NSTATE:] + dot(dyg_ref[...], state_bf),
        ],
        axis=1,
    ).astype(BF16)

    def token_grads():
        columns = cols_ref[...]
        pick_half = lanes8 // HEADDIM
        nt = ((1,), (1,))
        carried = jnp.zeros((8, TOK), F32)
        kept = jnp.zeros((8, TOK), F32)
        for pair in range(HEADS // 2):
            span = slice(128 * pair, 128 * pair + 128)
            picks = (rows8 == 2 * pair + pick_half).astype(BF16)
            top, rest = halves(dot(c_in, state_bf[span], nt) * dyg_ref[:, span].astype(F32))
            carried = carried + dot(picks, top, nt) + dot(picks, rest, nt)
            pulled = dot(b_in, gstate_bf[span], nt) * pair_columns(columns, 16, pair, low_half)
            top, rest = halves(pulled * x_ref[:, span].astype(F32))
            kept = kept + dot(picks, top, nt) + dot(picks, rest, nt)
            gx_ref[:, span] = gx_ref[:, span] + pulled
        grad_decay = jnp.sum(
            jnp.sum((state_in * grad_state).reshape(HEADS, HEADDIM, NSTATE), axis=1), axis=1, keepdims=True
        )
        end = jnp.sum(kept, axis=1, keepdims=True) + grad_decay * jnp.exp(last)
        token = lax.broadcasted_iota(jnp.int32, (8, TOK), 1)
        grad_cum = drow[...] - dcol[...] + carried - kept + jnp.where(token == TOK - 1, end, 0.0)
        tail = dot(grad_cum, (s_index >= t_index).astype(F32), precision=lax.Precision.HIGHEST)
        gstep_ref[...] = (dcol[...] + kept) / step - rate * tail
        grad_rate = -jnp.sum(step * tail, axis=1, keepdims=True)
        rate_row = jnp.sum(jnp.where(lanes8 == rows8, grad_rate, 0.0), axis=0, keepdims=True)
        few[0] = jnp.where(lane1 < HEADS, rate_row, skip_grads)

    order = (4, 3, 5, 2, 6, 1, 7, 0)

    def multiply(k):
        zz = (z + order[k]) % NZ
        for dx in range(NX):
            first_column = (((x + dx) % NX) * NZ + zz) * (NC * DEPTH)
            chunk = hid_t[pl.ds(pl.multiple_of(first_column, NC * DEPTH), NC * DEPTH)]
            prod[k, dx] = dot(chunk, grads).reshape(NC, DEPTH, COLS)
            mate_out[k, dx] = prod[k, dx, other].astype(BF16)
        send(mate_out, (k,), "m", ("m", k), mate, mate_in)

    def scale_of(block, seq_sums):
        one, two, three = starts
        chosen = jnp.where(block >= two, 2, 0)
        signed = jnp.where(lane1 == chosen, seq_sums, 0.0) - jnp.where(lane1 == chosen + 1, seq_sums, 0.0)
        margin = jnp.sum(signed, axis=1, keepdims=True)
        coef = 1.0 / (1.0 + jnp.exp(-hinge_sharp * (hinge_margin - margin)))
        rejected = ((block >= one) & (block < two)) | (block >= three)
        return jnp.where(rejected, coef, -coef)

    def combine(k):
        dz = order[k]
        arrive(mate_in, (k,), ("m", k))
        for dx in (2, 1, 3):
            both = prod[k, dx, c] * scale + mate_in[k, dx].astype(F32) * scale_mate
            a_out[k, dx - 1] = both[:PART].astype(BF16)
            send(a_out, (k, dx - 1), "a", ("a", k), to_x(dx), a_in)
            prod[k, dx, c, PART:] = both[PART:]
        both = prod[k, 0, c] * scale + mate_in[k, 0].astype(F32) * scale_mate
        a_own[k] = both[:PART]
        prod[k, 0, c, PART:] = both[PART:]
        if dz:
            b_out[k] = prod[k, :, c, PART:].astype(BF16)
            send(b_out, (k,), "b", "b", to_z(dz), bz_in)

    def pass_on(k):
        dz = order[k]
        arrive(a_in, (k,), ("a", k))
        a_own[k] = a_own[k] + jnp.sum(a_in[k].astype(F32), axis=0)
        if dz:
            a2_out[k] = a_own[k].astype(BF16)
            send(a2_out, (k,), "a2", "a2", to_z(dz), a2_in)

    for k in range(AHEAD):
        multiply(k)
    token_grads()
    settle_few(across, gr.at[1], 2 * NHEAD - 1)
    seq_sums = jnp.sum(across[...], axis=0)
    scale, scale_mate = scale_of(index, seq_sums), scale_of(index + 1 - 2 * c, seq_sums)
    few[0] = few[0] * scale
    move(few.at[0], few_c, "fc", "fc", mate)
    for k in range(NZ):
        combine(k)
        if k == 1:
            arrive(few_c, (every,), "fc")
            few[1] = few[0] + few_c[...]
            for j, (dx, dz) in enumerate(FAR_FIRST):
                move(few.at[1], few_all.at[j], "fz", "fz", at(x + dx, z + dz, c, head))
        if k + AHEAD < NZ:
            multiply(k + AHEAD)

    gx_bf[...] = (gx_ref[...] * scale).astype(BF16)
    gstep_ref[...] = gstep_ref[...] * scale
    stores = [
        pltpu.make_async_copy(gx_bf, grad_x_out, load_sem.at[0]),
        pltpu.make_async_copy(gstep_ref, grad_step_out, load_sem.at[1]),
    ]
    for store in stores:
        store.start()
    pass_on(0)
    for k in range(1, 4):
        pass_on(k)
    pass_on(4)
    b_sum = prod[NZ - 1, :, c, PART:]
    arrive(bz_in, (every,), "b")
    for k in range(NZ - 1):
        b_sum = b_sum + bz_in[k].astype(F32)
    for dx in (2, 1, 3):
        b2_out[dx - 1] = b_sum[dx].astype(BF16)
        send(b2_out, (dx - 1,), "b2", "b2", to_x(dx), b2_in)
    for k in range(5, NZ):
        pass_on(k)
    arrive(b2_in, (every,), "b2")
    gw_ref[PART:] = b_sum[0] + jnp.sum(b2_in[...].astype(F32), axis=0)
    a_sum = a_own[NZ - 1]
    arrive(few_all, (every,), "fz")
    small = few[1] + jnp.sum(few_all[...], axis=0)
    for h in range(HEADS):
        rate_ref[h] = small[0, h]
        skip_ref[h] = small[0, HEADS + h]
    stores.append(pltpu.make_async_copy(rate_ref, rate_out, load_sem.at[2]))
    stores.append(pltpu.make_async_copy(skip_ref, skip_out, load_sem.at[4]))
    stores[-2].start()
    stores[-1].start()
    arrive(a2_in, (every,), "a2")
    for k in range(NZ - 1):
        a_sum = a_sum + a2_in[k].astype(F32)
    gw_ref[:PART] = a_sum
    stores.append(pltpu.make_async_copy(gw_ref, grad_w_out, load_sem.at[3]))
    stores[-1].start()

    drain("plane", moves.at[pl.ds(0, NZ // 2), pl.ds(0, TOK - 8)])
    drain("mate", buf.at[:, :, c])
    drain("dz", dec.at[x, pl.ds(0, NZ - 1), c])
    drain("dx", dec.at[pl.ds(0, NX - 1), :, c])
    drain("dm", dec.at[:, :, c])
    drain("lg", lg)
    drain("st", states.at[c])
    drain("m", mate_out)
    drain("a", a_out)
    drain("b", b_out)
    drain("a2", a2_out)
    drain("b2", b2_out)
    drain("fc", few.at[0])
    drain("fz", few_all)
    assert not sent
    settle(msg, send_sem.at[0])
    settle(reply, send_sem.at[1])
    settle_few(near, gs.at[0], CHIPS - 1)
    settle_few(across, gs.at[1], 2 * NHEAD - 1)
    for store in stores:
        store.wait()


def whole(hidden, w_bc, x_act, logp_dir, step_size, rate, skip, mask, base, stretches):
    shape = jax.ShapeDtypeStruct
    rest = DEPTH - PART
    return pl.pallas_call(
        whole_kernel,
        name="whole",
        out_shape=(
            shape((TOK, WIDE), BF16),
            shape((8, TOK), F32),
            shape((HEADS,), F32),
            shape((HEADS,), F32),
            shape((DEPTH, COLS), F32),
        ),
        in_specs=[pl.BlockSpec(memory_space=SPACE)] * 10,
        out_specs=tuple([pl.BlockSpec(memory_space=SPACE)] * 5),
        scratch_shapes=[
            pltpu.VMEM((TOK, MODEL), BF16),
            pltpu.VMEM((TOK, WIDE), BF16),
            pltpu.VMEM((TOK, WIDE), BF16),
            pltpu.VMEM((8, TOK), F32),
            pltpu.SMEM((8,), F32),
            pltpu.SMEM((8,), F32),
            pltpu.VMEM((1, TOK), jnp.int32),
            pltpu.VMEM((1, TOK), F32),
            pltpu.SMEM((4,), jnp.int32),
            pltpu.VMEM((NX, NZ, NC, DEPTH, COLS), BF16),
            pltpu.VMEM((NX, NZ, NC, 1, 128), F32),
            pltpu.VMEM((HEADS, TOK, TOK), F32),
            pltpu.VMEM((HEADS, TOK, TOK), F32),
            pltpu.VMEM((128, TOK), F32),
            pltpu.VMEM((TOK, 128), F32),
            pltpu.VMEM((TOK, WIDE), BF16),
            pltpu.VMEM((TOK, WIDE), BF16),
            pltpu.VMEM((8, TOK), F32),
            pltpu.VMEM((8, TOK), F32),
            pltpu.VMEM((2, 2, WIDE // 2, NSTATE), F32),
            pltpu.VMEM((2, 2, WIDE // 2, NSTATE), F32),
            pltpu.VMEM((CHIPS, 16, 128), BF16),
            pltpu.VMEM((CHIPS, 16, 128), BF16),
            pltpu.VMEM((CHIPS, 16, 128), F32),
            pltpu.VMEM((CHIPS, 16, 128), F32),
            pltpu.VMEM((CHIPS, 16, 128), BF16),
            pltpu.VMEM((2, CHIPS, 16, 128), BF16),
            pltpu.VMEM((2, CHIPS, 128), F32),
            pltpu.VMEM((2, 1, 128), F32),
            pltpu.VMEM((CHIPS, 1, 128), F32),
            pltpu.VMEM((2 * NHEAD, 1, 128), F32),
            pltpu.VMEM((MODEL, TOK), BF16),
            pltpu.VMEM((WIDE, TOK), BF16),
            pltpu.VMEM((WIDE, TOK), BF16),
            pltpu.VMEM((TOK, WIDE), F32),
            pltpu.VMEM((TOK, COLS), F32),
            pltpu.VMEM((TOK, WIDE), BF16),
            pltpu.VMEM((8, TOK), F32),
            pltpu.VMEM((DEPTH, COLS), F32),
            pltpu.VMEM((NZ, NX, NC, DEPTH, COLS), F32),
            pltpu.VMEM((NZ, NX, DEPTH, COLS), BF16),
            pltpu.VMEM((NZ, NX, DEPTH, COLS), BF16),
            pltpu.VMEM((NZ, NX - 1, PART, COLS), BF16),
            pltpu.VMEM((NZ, PART, COLS), F32),
            pltpu.VMEM((NZ, NX - 1, PART, COLS), BF16),
            pltpu.VMEM((NZ - 1, PART, COLS), BF16),
            pltpu.VMEM((NZ - 1, PART, COLS), BF16),
            pltpu.VMEM((NZ - 1, NX, rest, COLS), BF16),
            pltpu.VMEM((NZ - 1, NX, rest, COLS), BF16),
            pltpu.VMEM((NX - 1, rest, COLS), BF16),
            pltpu.VMEM((NX - 1, rest, COLS), BF16),
            pltpu.VMEM((2, 1, 128), F32),
            pltpu.VMEM((1, 128), F32),
            pltpu.VMEM((CHIPS - 1, 1, 128), F32),
            pltpu.SemaphoreType.DMA((10,)),
            pltpu.SemaphoreType.DMA((2,)),
            pltpu.SemaphoreType.DMA((2,)),
            pltpu.SemaphoreType.DMA((14,)),
            pltpu.SemaphoreType.DMA((53,)),
            pltpu.SemaphoreType.DMA((2,)),
            pltpu.SemaphoreType.DMA((2,)),
        ],
        compiler_params=pltpu.CompilerParams(
            collective_id=0, has_side_effects=True, vmem_limit_bytes=VMEM_LIMIT
        ),
    )(hidden, w_bc, x_act, logp_dir, step_size, rate, skip, mask, base, stretches)


def finish_kernel(*refs):
    *ends, sems = refs
    count = len(ends) // 3
    steps = []
    for k in range(count):
        trio = ends[k], ends[2 * count + k], ends[count + k]
        rows = trio[0].shape[0]
        if rows > DEPTH:
            steps += [[ref.at[pl.ds(first, DEPTH)] for ref in trio] for first in range(0, rows, DEPTH)]
        else:
            steps.append(trio)
    into = [pltpu.make_async_copy(source, hold, sems.at[k]) for k, (source, hold, _) in enumerate(steps)]
    back = [
        pltpu.make_async_copy(hold, target, sems.at[len(steps) + k])
        for k, (_, hold, target) in enumerate(steps)
    ]
    for copy in into:
        copy.start()
    for arrived, copy in zip(into, back):
        arrived.wait()
        copy.start()
    for copy in back:
        copy.wait()


def finish(*arrays):
    spec = pl.BlockSpec(memory_space=SPACE)
    return pl.pallas_call(
        finish_kernel,
        name="finish",
        out_shape=tuple(jax.ShapeDtypeStruct(array.shape, array.dtype) for array in arrays),
        in_specs=[spec] * len(arrays),
        out_specs=tuple([spec] * len(arrays)),
        scratch_shapes=[
            (pltpu.VMEM if array.ndim == 2 else pltpu.SMEM)(array.shape, array.dtype) for array in arrays
        ]
        + [pltpu.SemaphoreType.DMA((2 * sum(max(1, array.shape[0] // DEPTH) for array in arrays),))],
        compiler_params=pltpu.CompilerParams(vmem_limit_bytes=VMEM_LIMIT),
    )(*arrays)


def body(
    hidden, w_bc, x_act, step_size, decay_rate, skip_gain, logp_dir, base_logp, seq_stretches, resp_mask
):
    return finish(
        *whole(
            hidden, w_bc, x_act, logp_dir, step_size, decay_rate, skip_gain,
            resp_mask.reshape(1, TOK), base_logp.reshape(1, TOK), seq_stretches,
        )
    )


def solution(mesh):
    return jax.shard_map(
        body,
        mesh=mesh,
        in_specs=(
            P("ctx", None),
            P("ctx", "head"),
            P("ctx", "head"),
            P("head", "ctx"),
            P("head"),
            P("head"),
            P("ctx", "head"),
            P("ctx"),
            P(),
            P("ctx"),
        ),
        out_specs=(P("ctx", "head"), P("head", "ctx"), P("head"), P("head"), P("ctx", "head")),
        check_vma=False,
    )
```
